256 devices in a mesh: img: 32 (over z_lo, y, core), txt: 8 (over z_hi, x).
Axes of the slice: x: 4, y: 4, z: 8 (z_hi: 2, z_lo: 4; z = z_hi * 4 + z_lo), core: 2. Of those that a mesh axis runs over, the one named last changes fastest.
Arguments:
- text_states: bfloat16 [512, 77, 1280], P(('img', 'txt')), may hold values from -6 to 6
- text_length: int32 [512], P(('img', 'txt')), may hold values from 1 to 77, as said below
- sample_count: int32 [256], P(('img', 'txt')), may hold values from 1 to 2, as said below
- mlp_gain: float32 [1280], replicated, may hold values from 0.1 to 1.9
- up_weight: bfloat16 [1280, 5120], P(None, 'txt'), may hold values from -0.15625 to 0.15625
- down_weight: bfloat16 [5120, 1280], P('txt'), may hold values from -0.078125 to 0.078125
- final_gain: float32 [1280], replicated, may hold values from 0.1 to 1.9
- text_proj: bfloat16 [1280, 1280], replicated, may hold values from -0.15625 to 0.15625
- image_pooled: bfloat16 [512, 1664], P(('img', 'txt')), may hold values from -6 to 6
- image_gain: float32 [1664], replicated, may hold values from 0.1 to 1.9
- image_proj: bfloat16 [1664, 1280], replicated, may hold values from -0.15625 to 0.15625
- logit_scale: float32 [], replicated, may hold values from 20 to 100
Outputs:
- image_proj_grad: float32 [1664, 1280], P('txt', 'img')
- up_grad: float32 [1280, 5120], P('img', 'txt')
- down_grad: float32 [5120, 1280], P('txt', 'img')
The draws below stay inside these ranges and needn't reach their ends.
Inputs may be any that keep to these rules, and one draw needn't show every extreme that they name: Text b has text_length[b] real tokens; the longest text has 77. Slot k of device d holds a real image and text pair exactly when k < sample_count[d]; some device has all 2 slots filled.
All inputs are finite; a program needn't handle non-finite values.
Results may differ from the reference program's by a relative error of at most 0.035.
Values may be sent and summed in bfloat16 or wider, within the bound.
No kernel may reach another device: no remote copies, remote signals or barrier semaphores. Data moves between devices by JAX's collectives and lax.ppermute only.
A program may use at most 128 MiB of HBM per device.

```python
import math
import jax
import jax.numpy as jnp
from jax import lax

DI = 1664
DT = 1280
FF = 5120
E = 1280
L = 77
S = 2
BATCH = 512
SHARDS = 256
N_IMG = 32
N_TXT = 8


def draw_text_length(key, part):
    key = jax.random.fold_in(key, 11)
    lengths = jax.random.randint(key, (BATCH,), 1, L + 1)
    return lengths.at[0].set(L).astype(jnp.int32)


def draw_sample_count(key, part):
    key = jax.random.fold_in(key, 23)
    counts = jax.random.randint(key, (SHARDS,), 1, S + 1)
    return counts.at[0].set(S).astype(jnp.int32)


def block_scale(key, dims, cuts, smallest, largest):
    factor_of, own = 1.0, jax.random.fold_in(key, 6)
    for position, shards_of in cuts:
        heights = jnp.exp(jax.random.uniform(jax.random.fold_in(own, position), (shards_of,), jnp.float32, smallest / len(cuts), largest / len(cuts)))
        factor_of = factor_of * jnp.repeat(heights, dims[position] // shards_of).reshape([-1 if axis == position else 1 for axis in range(len(dims))])
    return factor_of


def bell_draw(stream_key, dims, scale, limit, split=(), dtype=jnp.bfloat16):
    array = jax.random.normal(stream_key, dims, jnp.float32) * scale
    if len(split) > 0:
        array = block_scale(stream_key, dims, split, -0.22, 0.18) * array
    return jnp.clip(array, min=-limit, max=limit).astype(dtype)


def setup_inputs(seed: int = 0) -> dict:
    key_of = jax.random.split(jax.random.key(seed), 13)
    return {
        "text_states": bell_draw(key_of[0], (BATCH, L, DT), 1.0, 6.0, ((0, 256),)),
        "text_length": draw_text_length(jax.random.fold_in(key_of[12], 71), 0),
        "sample_count": draw_sample_count(jax.random.fold_in(key_of[12], 71), 0),
        "mlp_gain": jnp.clip(1.0 + 0.18 * jax.random.normal(key_of[3], (DT,), jnp.float32), 0.1, 1.9),
        "up_weight": bell_draw(key_of[4], (DT, FF), DT ** -0.5, 0.15625, ((1, 8),)),
        "down_weight": bell_draw(key_of[5], (FF, DT), FF ** -0.5, 0.078125, ((0, 8),)),
        "final_gain": jnp.clip(1.0 + 0.18 * jax.random.normal(key_of[6], (DT,), jnp.float32), 0.1, 1.9),
        "text_proj": bell_draw(key_of[7], (DT, E), DT ** -0.5, 0.15625),
        "image_pooled": bell_draw(key_of[8], (BATCH, DI), 1.0, 6.0, ((0, 256),)),
        "image_gain": jnp.clip(1.0 + 0.18 * jax.random.normal(key_of[9], (DI,), jnp.float32), 0.1, 1.9),
        "image_proj": bell_draw(key_of[10], (DI, E), DI ** -0.5, 0.15625),
        "logit_scale": jnp.clip(jnp.exp(jax.random.uniform(key_of[11], (), jnp.float32, math.log(20.0), math.log(100.0))), 20.0, 100.0),
    }


EPSILON = 1e-05
ROOT_HALF = 0.7071067811865476
INV_ROOT_TAU = 0.3989422804014327

def gelu_exact(value):
    return 0.5 * value * (1.0 + lax.erf(value * ROOT_HALF))

def gelu_slope(value):
    return 0.5 * (1.0 + lax.erf(value * ROOT_HALF)) + value * INV_ROOT_TAU * jnp.exp(-0.5 * value * value)

def norm_parts(values):
    centred = values - lax.optimization_barrier(jnp.mean(values, axis=-1, keepdims=True))
    inv_std = lax.rsqrt(lax.optimization_barrier(jnp.mean(centred * centred, axis=-1, keepdims=True)) + EPSILON)
    return (centred * inv_std, inv_std)

def unit_rows(raw):
    inv_norm = lax.rsqrt(lax.optimization_barrier(jnp.sum(raw * raw, axis=-1, keepdims=True)) + 1e-06)
    return (raw * inv_norm, inv_norm)

def unit_back(grad_unit, direction, inv_norm):
    return inv_norm * (grad_unit - direction * lax.optimization_barrier(jnp.sum(direction * grad_unit, axis=-1, keepdims=True)))

def masked_logsum(scores, keep_mask):
    row_top = lax.optimization_barrier(jnp.max(jnp.where(keep_mask, scores, -1e+30), axis=-1, keepdims=True))
    summed = lax.optimization_barrier(jnp.sum(jnp.exp(jnp.where(keep_mask, scores - row_top, -1e+30)), axis=-1, keepdims=True))
    return (row_top + jnp.log(summed))[:, 0]

def text_forward(states, lengths, mlp_gain, up_weight, down_weight, final_gain):
    samples, length, model_width = states.shape
    states_flat = states.reshape(samples * length, model_width).astype(jnp.float32)
    scaled, _ = norm_parts(states_flat)
    normed = (scaled * mlp_gain).astype(jnp.bfloat16)
    preact = jnp.dot(normed, up_weight, preferred_element_type=jnp.float32)
    activation = gelu_exact(preact).astype(jnp.bfloat16)
    hidden = states_flat + jnp.dot(activation, down_weight, preferred_element_type=jnp.float32)
    final_hat, final_inv = norm_parts(hidden)
    keep_mask = (jnp.arange(length)[None, :] < lengths[:, None]).astype(jnp.float32)
    weights = keep_mask / lengths[:, None].astype(jnp.float32)
    final_rows = (final_hat * final_gain).reshape(samples, length, model_width)
    pooled = lax.optimization_barrier(jnp.sum(final_rows * weights[:, :, None], axis=1)).astype(jnp.bfloat16)
    return (pooled, (normed, preact, activation, final_hat, final_inv, weights))

def text_backward(grad_pooled, saved_parts, down_weight, final_gain):
    normed, preact, activation, final_hat, final_inv, weights = saved_parts
    samples, length = weights.shape
    grad_final = (grad_pooled[:, None, :] * weights[:, :, None]).reshape(samples * length, -1)
    scaled_grad = grad_final * final_gain
    grad_hidden = final_inv * (scaled_grad - lax.optimization_barrier(jnp.mean(scaled_grad, axis=-1, keepdims=True)) - final_hat * lax.optimization_barrier(jnp.mean(scaled_grad * final_hat, axis=-1, keepdims=True)))
    grad_hidden = grad_hidden.astype(jnp.bfloat16)
    down_part = jnp.dot(activation.T, grad_hidden, preferred_element_type=jnp.float32)
    grad_act = jnp.dot(grad_hidden, down_weight.T, preferred_element_type=jnp.float32)
    grad_preact = (grad_act * gelu_slope(preact)).astype(jnp.bfloat16)
    up_part = jnp.dot(normed.T, grad_preact, preferred_element_type=jnp.float32)
    return (up_part, down_part)

def reference(text_states, text_length, sample_count, mlp_gain, up_weight, down_weight, final_gain, text_proj, image_pooled, image_gain, image_proj, logit_scale):
    group_size = S * N_TXT
    state_blocks = text_states.reshape(N_IMG, group_size, L, DT)
    length_blocks = text_length.reshape(N_IMG, group_size)

    def pool_block(pieces):
        return text_forward(pieces[0], pieces[1], mlp_gain, up_weight, down_weight, final_gain)[0]
    pooled = lax.map(pool_block, (state_blocks, length_blocks)).reshape(BATCH, DT)
    text_raw = jnp.dot(pooled, text_proj, preferred_element_type=jnp.float32)
    text_unit, text_inv = unit_rows(text_raw)
    text_send = text_unit.astype(jnp.bfloat16)
    image_scaled, _ = norm_parts(image_pooled.astype(jnp.float32))
    image_normed = (image_scaled * image_gain).astype(jnp.bfloat16)
    image_raw = jnp.dot(image_normed, image_proj, preferred_element_type=jnp.float32)
    image_unit, image_inv = unit_rows(image_raw)
    image_send = image_unit.astype(jnp.bfloat16)
    slots = jnp.arange(BATCH) % S
    valid = slots < jnp.repeat(sample_count, S)
    scores = logit_scale * jnp.dot(image_send, text_send.T, preferred_element_type=jnp.float32)
    row_lse = masked_logsum(scores, valid[None, :])
    col_lse = masked_logsum(scores.T, valid[None, :])
    pair_mask = valid[:, None] & valid[None, :]
    same_index = jnp.arange(BATCH)[:, None] == jnp.arange(BATCH)[None, :]
    row_prob = jnp.exp(jnp.where(pair_mask, scores - row_lse[:, None], -1e+30))
    col_prob = jnp.exp(jnp.where(pair_mask, scores - col_lse[None, :], -1e+30))
    grad_scores = 0.5 * (row_prob + col_prob) - jnp.where(pair_mask & same_index, 1.0, 0.0)
    grad_image_unit = logit_scale * jnp.dot(grad_scores, text_send.astype(jnp.float32), precision=lax.Precision.HIGHEST)
    grad_text_unit = logit_scale * jnp.dot(grad_scores.T, image_send.astype(jnp.float32), precision=lax.Precision.HIGHEST)
    grad_image_raw = unit_back(grad_image_unit, image_unit, image_inv).astype(jnp.bfloat16)
    grad_text_raw = unit_back(grad_text_unit, text_unit, text_inv).astype(jnp.bfloat16)
    image_proj_grad = jnp.dot(image_normed.T, grad_image_raw, preferred_element_type=jnp.float32)
    grad_pooled = jnp.dot(grad_text_raw, text_proj.T, preferred_element_type=jnp.float32)
    grad_blocks = grad_pooled.reshape(N_IMG, group_size, DT)

    def block_grads(running, pieces):
        _, saved_parts = text_forward(pieces[0], pieces[1], mlp_gain, up_weight, down_weight, final_gain)
        up_part, down_part = text_backward(pieces[2], saved_parts, down_weight, final_gain)
        up_round = lax.optimization_barrier(up_part.astype(jnp.bfloat16))
        down_round = lax.optimization_barrier(down_part.astype(jnp.bfloat16))
        return ((running[0] + up_round.astype(jnp.float32), running[1] + down_round.astype(jnp.float32)), None)
    start_sums = (jnp.zeros((DT, FF), jnp.float32), jnp.zeros((FF, DT), jnp.float32))
    (up_grad, down_grad), _ = lax.scan(block_grads, start_sums, (state_blocks, length_blocks, grad_blocks))
    return (image_proj_grad, up_grad, down_grad)
```

```python
import jax
import jax.numpy as jnp
from jax import lax
from jax.sharding import PartitionSpec as P

EPSILON = 1e-05
ROOT_HALF = 0.7071067811865476
INV_ROOT_TAU = 0.3989422804014327
BF = jnp.bfloat16
F32 = jnp.float32
PAD = 80


def gelu_exact(value):
    return 0.5 * value * (1.0 + lax.erf(value * ROOT_HALF))


def gelu_slope(value):
    return 0.5 * (1.0 + lax.erf(value * ROOT_HALF)) + value * INV_ROOT_TAU * jnp.exp(
        -0.5 * value * value
    )


def centre(values):
    return values - jnp.mean(values, axis=-1, keepdims=True)


def inv_std_of(centred):
    return lax.rsqrt(jnp.mean(centred * centred, axis=-1, keepdims=True) + EPSILON)


def unit_rows(raw):
    inv_norm = lax.rsqrt(jnp.sum(raw * raw, axis=-1, keepdims=True) + 1e-06)
    return (raw * inv_norm, inv_norm)


def unit_back(grad_unit, direction, inv_norm):
    return inv_norm * (
        grad_unit - direction * jnp.sum(direction * grad_unit, axis=-1, keepdims=True)
    )


def move_txt(value, z_hi=0, x=0):
    pairs = [
        (a * 4 + b, ((a + z_hi) % 2) * 4 + (b + x) % 4) for a in range(2) for b in range(4)
    ]
    return lax.ppermute(value, "txt", pairs)


def move_img(value, z_lo=0, y=0, core=0):
    pairs = [
        (a * 8 + b * 2 + c, ((a + z_lo) % 4) * 8 + ((b + y) % 4) * 2 + (c + core) % 2)
        for a in range(4)
        for b in range(4)
        for c in range(2)
    ]
    return lax.ppermute(value, "img", pairs)


def four(value, move):
    return jnp.concatenate([value, move(value, 1), move(value, -1), move(value, 2)], axis=0)


def gather_rows(rows):
    rows = lax.optimization_barrier(four(rows, lambda v, k: move_txt(v, x=k)))
    rows = lax.optimization_barrier(jnp.concatenate([rows, move_txt(rows, z_hi=1)], axis=0))
    rows = lax.optimization_barrier(four(rows, lambda v, k: move_img(v, z_lo=k)))
    rows = lax.optimization_barrier(four(rows, lambda v, k: move_img(v, y=k)))
    return jnp.concatenate([rows, move_img(rows, core=1)], axis=0)


def ring_x(piece):
    half = piece.shape[0] // 2
    from_left = move_txt(piece, x=1)
    from_right = move_txt(piece, x=-1)
    far_a = move_txt(from_left[:half], x=1)
    far_b = move_txt(from_right[half:], x=-1)
    return jnp.concatenate([piece, from_left, from_right, far_a, far_b], axis=0)


def ring_x_sum(terms):
    rows = terms.shape[0] // 4
    half = rows // 2
    own, left, right, far = (terms[k * rows : (k + 1) * rows] for k in range(4))
    for_right = move_txt(far[:half].astype(BF), x=1).astype(F32)
    for_left = move_txt(far[half:].astype(BF), x=-1).astype(F32)
    right = jnp.concatenate([right[:half] + for_right, right[half:]], axis=0)
    left = jnp.concatenate([left[:half], left[half:] + for_left], axis=0)
    from_left = move_txt(right.astype(BF), x=1)
    from_right = move_txt(left.astype(BF), x=-1)
    return own + from_left.astype(F32) + from_right.astype(F32)


def pick(value, index, axis):
    return lax.dynamic_index_in_dim(value, index, axis, keepdims=False)


def sum_img(terms, z_lo, y, core):
    blocks = terms.reshape(4, 4, 2, terms.shape[0] // 32, terms.shape[1])
    got = move_img(pick(blocks, 1 - core, 2).astype(BF), core=1)
    blocks = pick(blocks, core, 2) + got.astype(F32)
    total = pick(blocks, y, 1)
    for k in (2, 1, -1):
        total = total + move_img(pick(blocks, (y + k) % 4, 1).astype(BF), y=k).astype(F32)
    blocks = total
    total = pick(blocks, z_lo, 0)
    for k in (2, 1, -1):
        total = total + move_img(pick(blocks, (z_lo + k) % 4, 0).astype(BF), z_lo=k).astype(F32)
    return total


def body(
    text_states,
    text_length,
    sample_count,
    mlp_gain,
    up_weight,
    down_weight,
    final_gain,
    text_proj,
    image_pooled,
    image_gain,
    image_proj,
    logit_scale,
):
    samples, length, width = text_states.shape
    image_width = image_pooled.shape[1]
    txt = lax.axis_index("txt")
    img = lax.axis_index("img")
    z_lo, y, core = img // 8, (img // 2) % 4, img % 2

    states = jnp.pad(text_states, ((0, 0), (0, PAD - length), (0, 0)))
    states = states.reshape(samples * PAD, width).astype(F32)
    centred = centre(states)
    normed_own = (centred * inv_std_of(centred) * mlp_gain).astype(BF)
    normed_far = move_txt(normed_own, z_hi=1)

    valid_own = (jnp.arange(samples) < sample_count[0]).astype(BF)
    extra = jnp.stack([valid_own, text_length.astype(BF)], axis=1)
    image_rows = jnp.concatenate(
        [image_pooled, jnp.pad(extra, ((0, 0), (0, 126)))], axis=1
    )

    normed_near = ring_x(normed_own)
    normed_away = ring_x(normed_far)
    image_rows, _ = lax.optimization_barrier((image_rows, normed_away))
    image_all = gather_rows(image_rows)

    def forward(normed):
        preact = jnp.dot(normed, up_weight, preferred_element_type=F32)
        activation = gelu_exact(preact).astype(BF)
        slope = gelu_slope(preact).astype(BF)
        activation, slope = lax.optimization_barrier((activation, slope))
        return slope, activation, jnp.dot(activation, down_weight, preferred_element_type=F32)

    slope_near, act_near, out_near = forward(normed_near)
    slope_away, act_away, out_away = forward(normed_away)
    from_away = move_txt(ring_x_sum(out_away).astype(BF), z_hi=1)
    hidden = states + ring_x_sum(out_near) + from_away.astype(F32)

    hidden_centred = centre(hidden)
    final_hat = hidden_centred * inv_std_of(hidden_centred)
    keep_mask = (jnp.arange(PAD)[None, :] < text_length[:, None]).astype(F32)
    weights_own = keep_mask / text_length[:, None].astype(F32)
    final_rows = (final_hat * final_gain).reshape(samples, PAD, width)
    pooled = jnp.sum(final_rows * weights_own[:, :, None], axis=1).astype(BF)
    pooled_all = gather_rows(pooled)
    hidden_send = hidden_centred.astype(BF)
    hidden_far = move_txt(hidden_send, z_hi=1)
    hidden_near = ring_x(hidden_send)
    hidden_far, _ = lax.optimization_barrier((hidden_far, pooled_all))
    hidden_group = jnp.concatenate([hidden_near, ring_x(hidden_far)], axis=0).astype(F32)
    group_inv = inv_std_of(hidden_group)

    valid = image_all[:, image_width] > 0.5
    lengths = image_all[: 8 * samples, image_width + 1].astype(F32)
    image_centred = centre(image_all[:, :image_width].astype(F32))
    image_normed = (image_centred * inv_std_of(image_centred) * image_gain).astype(BF)
    image_raw = jnp.dot(image_normed, image_proj, preferred_element_type=F32)
    image_unit, image_inv = unit_rows(image_raw)
    image_send = image_unit.astype(BF)

    text_raw = jnp.dot(pooled_all, text_proj, preferred_element_type=F32)
    text_unit, text_inv = unit_rows(text_raw)
    text_send = text_unit.astype(BF)
    scores = logit_scale * lax.dot_general(
        image_send, text_send, (((1,), (1,)), ((), ())), preferred_element_type=F32
    )
    batch = scores.shape[0]

    def masked_logsum(axis, mask):
        top = jnp.max(jnp.where(mask, scores, -1e30), axis=axis, keepdims=True)
        total = jnp.sum(jnp.exp(jnp.where(mask, scores - top, -1e30)), axis=axis, keepdims=True)
        return top + jnp.log(total)

    row_lse = masked_logsum(1, valid[None, :])
    col_lse = masked_logsum(0, valid[:, None])
    pair_mask = valid[:, None] & valid[None, :]
    row_prob = jnp.exp(jnp.where(pair_mask, scores - row_lse, -1e30))
    col_prob = jnp.exp(jnp.where(pair_mask, scores - col_lse, -1e30))
    same = jnp.arange(batch)[:, None] == jnp.arange(batch)[None, :]
    grad_scores = 0.5 * (row_prob + col_prob) - jnp.where(pair_mask & same, 1.0, 0.0)
    grad_high = lax.reduce_precision(grad_scores, 8, 7)
    grad_low = (grad_scores - grad_high).astype(BF)
    grad_high = grad_high.astype(BF)

    group = 8 * samples
    dims = (((0,), (0,)), ((), ()))
    grad_text_unit = logit_scale * (
        lax.dot_general(grad_high[:, :group], image_send, dims, preferred_element_type=F32)
        + lax.dot_general(grad_low[:, :group], image_send, dims, preferred_element_type=F32)
    )
    grad_text_raw = unit_back(grad_text_unit, text_unit[:group], text_inv[:group]).astype(BF)
    grad_pooled = lax.dot_general(
        grad_text_raw, text_proj, (((1,), (1,)), ((), ())), preferred_element_type=F32
    )
    keep_group = (jnp.arange(PAD)[None, :] < lengths[:, None]).astype(F32)
    weights = (keep_group / lengths[:, None])[:, :, None]
    scaled = (grad_pooled * final_gain)[:, None, :]
    group_hat = (hidden_group * group_inv).reshape(group, PAD, width)
    grad_hidden = (
        group_inv.reshape(group, PAD, 1)
        * weights
        * (
            scaled
            - jnp.mean(scaled, axis=-1, keepdims=True)
            - group_hat * jnp.mean(scaled * group_hat, axis=-1, keepdims=True)
        )
    )
    grad_hidden = grad_hidden.reshape(group * PAD, width).astype(BF)

    normed = jnp.concatenate([normed_near, normed_away], axis=0)
    activation = jnp.concatenate([act_near, act_away], axis=0)
    slope = jnp.concatenate([slope_near, slope_away], axis=0)
    down_terms = lax.dot_general(grad_hidden, activation, dims, preferred_element_type=F32)
    down_grad = sum_img(down_terms, z_lo, y, core).T
    grad_act = lax.dot_general(
        grad_hidden, down_weight, (((1,), (1,)), ((), ())), preferred_element_type=F32
    )
    grad_preact = lax.optimization_barrier((grad_act * slope.astype(F32)).astype(BF))
    up_terms = lax.dot_general(normed, grad_preact, dims, preferred_element_type=F32)
    up_grad = sum_img(up_terms, z_lo, y, core)

    grad_image_unit = logit_scale * (
        jnp.dot(grad_high, text_send, preferred_element_type=F32)
        + jnp.dot(grad_low, text_send, preferred_element_type=F32)
    )
    grad_image_raw = unit_back(grad_image_unit, image_unit, image_inv).astype(BF)
    columns = grad_image_raw.shape[1] // 32
    chosen = jnp.arange(grad_image_raw.shape[1])[:, None] == (
        img * columns + jnp.arange(columns)[None, :]
    )
    own_columns = jnp.dot(
        grad_image_raw, chosen.astype(BF), preferred_element_type=F32
    ).astype(BF)
    projected = lax.dot_general(image_normed, own_columns, dims, preferred_element_type=F32)
    rows = image_width // 8
    image_proj_grad = lax.dynamic_slice_in_dim(projected, txt * rows, rows, axis=0)
    return (image_proj_grad, up_grad, down_grad)


def solution(mesh):
    return jax.shard_map(
        body,
        mesh=mesh,
        in_specs=(
            P(("img", "txt"), None, None),
            P(("img", "txt")),
            P(("img", "txt")),
            P(),
            P(None, "txt"),
            P("txt", None),
            P(),
            P(),
            P(("img", "txt"), None),
            P(),
            P(),
            P(),
        ),
        out_specs=(P("txt", "img"), P("img", "txt"), P("txt", "img")),
        check_vma=False,
    )
```

```python
import jax
import jax.numpy as jnp
from jax import lax
from jax.experimental import pallas as pl
from jax.experimental.pallas import tpu as pltpu
from jax.sharding import PartitionSpec as P

EPSILON = 1e-05
ROOT_HALF = 0.7071067811865476
INV_ROOT_TAU = 0.3989422804014327
BF = jnp.bfloat16
F32 = jnp.float32
PAD = 80


def centre(values):
    return values - jnp.mean(values, axis=-1, keepdims=True)


def inv_std_of(centred):
    return lax.rsqrt(jnp.mean(centred * centred, axis=-1, keepdims=True) + EPSILON)


def unit_rows(raw):
    inv_norm = lax.rsqrt(jnp.sum(raw * raw, axis=-1, keepdims=True) + 1e-06)
    return (raw * inv_norm, inv_norm)


def unit_back(grad_unit, direction, inv_norm):
    return inv_norm * (
        grad_unit - direction * jnp.sum(direction * grad_unit, axis=-1, keepdims=True)
    )


VMEM_LIMIT = 40 * 1024 * 1024
OVER_ROWS = (((0,), (0,)), ((), ()))
OVER_COLS = (((1,), (1,)), ((), ()))


def call(kernel, outs, *operands, scratch=(), smem=0, flops=0):
    size = sum(v.size * v.dtype.itemsize for v in operands) + sum(
        v.size * v.dtype.itemsize for v in outs
    )
    specs = [pl.BlockSpec(memory_space=pltpu.SMEM)] * smem
    specs += [pl.BlockSpec(memory_space=pltpu.VMEM)] * (len(operands) - smem)
    return pl.pallas_call(
        kernel,
        out_shape=outs,
        in_specs=specs,
        out_specs=[pl.BlockSpec(memory_space=pltpu.VMEM)] * len(outs),
        scratch_shapes=list(scratch),
        cost_estimate=pl.CostEstimate(flops=flops, bytes_accessed=size, transcendentals=0),
        compiler_params=pltpu.CompilerParams(vmem_limit_bytes=VMEM_LIMIT),
    )(*operands)


def shape(rows, cols, dtype):
    return jax.ShapeDtypeStruct((rows, cols), dtype)


def padded(states_ref, slot, scratch):
    length = states_ref.shape[1]
    scratch[PAD - 8 :, :] = jnp.zeros((8, scratch.shape[1]), F32)
    scratch[:length, :] = states_ref[slot].astype(F32)
    return scratch[...]


def norm_kernel(states_ref, gain_ref, out_ref, scratch):
    for slot in range(states_ref.shape[0]):
        centred = centre(padded(states_ref, slot, scratch))
        scaled = centred * inv_std_of(centred) * gain_ref[...]
        out_ref[slot * PAD : (slot + 1) * PAD, :] = scaled.astype(BF)


def forward_kernel(
    own_ref, left_ref, right_ref, far_a_ref, far_b_ref, up_ref, down_ref,
    normed_ref, act_ref, slope_ref, o_own, o_left, o_right, o_far_a, o_far_b,
):
    place = 0
    for ref in (own_ref, left_ref, right_ref, far_a_ref, far_b_ref):
        normed_ref[place : place + ref.shape[0], :] = ref[...]
        place += ref.shape[0]
    half = place // 2
    rows = half // 2
    for part in range(2):
        span = slice(part * half, (part + 1) * half)
        preact = jnp.dot(normed_ref[span, :], up_ref[...], preferred_element_type=F32)
        cdf = 0.5 * (1.0 + lax.erf(preact * ROOT_HALF))
        act_ref[span, :] = (preact * cdf).astype(BF)
        slope = cdf + preact * INV_ROOT_TAU * jnp.exp(-0.5 * preact * preact)
        slope_ref[span, :] = slope.astype(BF)
        out = jnp.dot(act_ref[span, :], down_ref[...], preferred_element_type=F32)
        if part == 0:
            o_own[...] = out[:rows]
            o_left[...] = out[rows:]
        else:
            o_right[...] = out[:rows]
            o_far_a[...] = out[rows : rows + rows // 2].astype(BF)
            o_far_b[...] = out[rows + rows // 2 :].astype(BF)


def relay_kernel(left_ref, right_ref, got_a_ref, got_b_ref, o_left, o_right):
    half = got_a_ref.shape[0]
    o_right[:half, :] = (right_ref[:half, :] + got_a_ref[...].astype(F32)).astype(BF)
    o_right[half:, :] = right_ref[half:, :].astype(BF)
    o_left[:half, :] = left_ref[:half, :].astype(BF)
    o_left[half:, :] = (left_ref[half:, :] + got_b_ref[...].astype(F32)).astype(BF)


def final_kernel(
    length_ref, states_ref, own_ref, left_ref, right_ref, away_ref, gain_ref,
    pooled_ref, centred_ref, scratch,
):
    pooled = []
    for slot in range(states_ref.shape[0]):
        span = slice(slot * PAD, (slot + 1) * PAD)
        total = own_ref[span, :] + left_ref[span, :].astype(F32) + right_ref[span, :].astype(F32)
        total = total + away_ref[span, :].astype(F32)
        centred = centre(padded(states_ref, slot, scratch) + total)
        centred_ref[span, :] = centred.astype(BF)
        count = length_ref[slot]
        kept = (lax.broadcasted_iota(jnp.int32, (PAD, 1), 0) < count).astype(F32)
        weight = kept * inv_std_of(centred) / count.astype(F32)
        pooled.append(jnp.sum(centred * weight, axis=0, keepdims=True) * gain_ref[...])
    pooled_ref[...] = jnp.concatenate(pooled, axis=0).astype(BF)


def split_core(core, rows, part, send_ref, keep_ref):
    run = 40
    for j in range(rows.shape[0] // (4 * run)):
        first = rows[j * 4 * run : j * 4 * run + run]
        second = rows[j * 4 * run + run : j * 4 * run + 2 * run]
        third = rows[j * 4 * run + 2 * run : j * 4 * run + 3 * run]
        fourth = rows[j * 4 * run + 3 * run : j * 4 * run + 4 * run]
        even = jnp.concatenate([first, third], axis=0)
        odd = jnp.concatenate([second, fourth], axis=0)
        base = part * rows.shape[0] // 2 + j * 2 * run
        span = slice(base, base + 2 * run)
        send_ref[span, :] = jnp.where(core == 0, odd, even).astype(BF)
        keep_ref[span, :] = jnp.where(core == 0, even, odd)


def hidden_kernel(
    core_ref, length_ref, h0, h1, h2, h3, h4, h5, h6, h7, h8, h9, pulled_ref, act_a_ref, act_b_ref,
    grad_ref, send_ref, keep_ref,
):
    place = 0
    for ref in (h0, h1, h2, h3, h4, h5, h6, h7, h8, h9):
        grad_ref[place : place + ref.shape[0], :] = ref[...]
        place += ref.shape[0]

    def sample(index, carry):
        span = pl.ds(pl.multiple_of(index * PAD, PAD), PAD)
        centred = grad_ref[span, :].astype(F32)
        inv = inv_std_of(centred)
        hat = centred * inv
        pulled = pulled_ref[pl.ds(index, 1), :]
        along = jnp.mean(pulled * hat, axis=-1, keepdims=True)
        count = length_ref[index]
        kept = (lax.broadcasted_iota(jnp.int32, (PAD, 1), 0) < count).astype(F32)
        weight = kept * inv / count.astype(F32)
        grad = weight * (pulled - jnp.mean(pulled, axis=-1, keepdims=True) - hat * along)
        grad_ref[span, :] = grad.astype(BF)
        return carry

    lax.fori_loop(0, place // PAD, sample, 0)
    tokens = act_a_ref.shape[0]
    for part in range(2):
        cols = slice(part * 640, (part + 1) * 640)
        rows = lax.dot_general(
            grad_ref[:tokens, cols], act_a_ref[...], OVER_ROWS, preferred_element_type=F32
        ) + lax.dot_general(
            grad_ref[tokens:, cols], act_b_ref[...], OVER_ROWS, preferred_element_type=F32
        )
        split_core(core_ref[0], rows, part, send_ref, keep_ref)


def weights_kernel(
    core_ref, grad_ref, down_ref, slope_a_ref, slope_b_ref, normed_a_ref, normed_b_ref,
    send_ref, keep_ref, scratch,
):
    tokens = slope_a_ref.shape[0]
    for part, slope_ref in enumerate((slope_a_ref, slope_b_ref)):
        span = slice(part * tokens, (part + 1) * tokens)
        back = lax.dot_general(
            grad_ref[span, :], down_ref[...], OVER_COLS, preferred_element_type=F32
        )
        scratch[span, :] = (back * slope_ref[...].astype(F32)).astype(BF)
    for part in range(2):
        cols = slice(part * 640, (part + 1) * 640)
        rows = lax.dot_general(
            normed_a_ref[:, cols], scratch[:tokens, :], OVER_ROWS, preferred_element_type=F32
        ) + lax.dot_general(
            normed_b_ref[:, cols], scratch[tokens:, :], OVER_ROWS, preferred_element_type=F32
        )
        split_core(core_ref[0], rows, part, send_ref, keep_ref)


def spread_y_kernel(y_ref, keep_ref, got_ref, own_ref, s1_ref, s2_ref, s3_ref, scratch):
    scratch[...] = keep_ref[...] + got_ref[...].astype(F32)
    for shift, ref in ((0, own_ref), (1, s1_ref), (3, s2_ref), (2, s3_ref)):
        place = lax.rem(y_ref[0] + shift, 4) * 40
        for pair in range(2):
            runs = [
                scratch[pl.ds(pl.multiple_of((2 * pair + k) * 160 + place, 8), 40), :]
                for k in range(2)
            ]
            ref[pair * 80 : (pair + 1) * 80, :] = jnp.concatenate(runs, axis=0).astype(ref.dtype)


def spread_z_kernel(z_ref, keep_ref, r1_ref, r2_ref, r3_ref, own_ref, s1_ref, s2_ref, s3_ref, scratch):
    scratch[...] = (
        keep_ref[...]
        + r1_ref[...].astype(F32)
        + r2_ref[...].astype(F32)
        + r3_ref[...].astype(F32)
    )
    for shift, ref in ((0, own_ref), (1, s1_ref), (3, s2_ref), (2, s3_ref)):
        place = lax.rem(z_ref[0] + shift, 4) * 40
        ref[...] = scratch[pl.ds(pl.multiple_of(place, 8), 40), :].astype(ref.dtype)


def move_txt(value, z_hi=0, x=0):
    pairs = [
        (a * 4 + b, ((a + z_hi) % 2) * 4 + (b + x) % 4) for a in range(2) for b in range(4)
    ]
    return lax.ppermute(value, "txt", pairs)


def move_img(value, z_lo=0, y=0, core=0):
    pairs = [
        (a * 8 + b * 2 + c, ((a + z_lo) % 4) * 8 + ((b + y) % 4) * 2 + (c + core) % 2)
        for a in range(4)
        for b in range(4)
        for c in range(2)
    ]
    return lax.ppermute(value, "img", pairs)


def after(value, *events):
    return lax.optimization_barrier((value,) + events)[0]


def four(value, move):
    rows = [value, move(value, 1), move(value, -1), move(value, 2)]
    return lax.optimization_barrier(jnp.concatenate(rows, axis=0))


def gather_txt(rows):
    rows = four(rows, lambda v, k: move_txt(v, x=k))
    return lax.optimization_barrier(jnp.concatenate([rows, move_txt(rows, z_hi=1)], axis=0))


def gather_z(rows):
    return four(rows, lambda v, k: move_img(v, z_lo=k))


def gather_y(rows):
    return four(rows, lambda v, k: move_img(v, y=k))


def gather_core(rows):
    return jnp.concatenate([rows, move_img(rows, core=1)], axis=0)


def forward(pieces, up_weight, down_weight):
    tokens = 4 * pieces[0].shape[0]
    width, units = up_weight.shape
    rows = tokens // 4
    return call(
        forward_kernel,
        (
            shape(tokens, width, BF),
            shape(tokens, units, BF),
            shape(tokens, units, BF),
            shape(rows, width, F32),
            shape(rows, width, F32),
            shape(rows, width, F32),
            shape(rows // 2, width, BF),
            shape(rows // 2, width, BF),
        ),
        *pieces,
        up_weight,
        down_weight,
        flops=4 * tokens * width * units,
    )


def ring_sum_start(terms):
    _, left, right, far_a, far_b = terms
    got_a = move_txt(far_a, x=1)
    got_b = move_txt(far_b, x=-1)
    rows, width = left.shape
    left, right = call(
        relay_kernel, (shape(rows, width, BF),) * 2, left, right, got_a, got_b
    )
    return move_txt(right, x=1), move_txt(left, x=-1)


def sum_img(send, keep, z_lo, y):
    got = move_img(send, core=1)
    cols = keep.shape[1]
    outs = (shape(160, cols, F32),) + (shape(160, cols, BF),) * 3
    own, s1, s2, s3 = call(
        spread_y_kernel, outs, y, keep, got, scratch=[pltpu.VMEM(keep.shape, F32)], smem=1
    )
    s3, s1, s2 = move_img(s3, y=2), move_img(s1, y=1), move_img(s2, y=-1)
    outs = (shape(40, cols, F32),) + (shape(40, cols, BF),) * 3
    own, s1, s2, s3 = call(
        spread_z_kernel, outs, z_lo, own, s1, s2, s3,
        scratch=[pltpu.VMEM((160, cols), F32)], smem=1,
    )
    s3, s1, s2 = move_img(s3, z_lo=2), move_img(s1, z_lo=1), move_img(s2, z_lo=-1)
    return own + s1.astype(F32) + s2.astype(F32) + s3.astype(F32)


def body(
    text_states,
    text_length,
    sample_count,
    mlp_gain,
    up_weight,
    down_weight,
    final_gain,
    text_proj,
    image_pooled,
    image_gain,
    image_proj,
    logit_scale,
):
    samples, length, width = text_states.shape
    image_width = image_pooled.shape[1]
    txt = lax.axis_index("txt")
    img = lax.axis_index("img")
    z_lo, y, core = img // 8, (img // 2) % 4, img % 2

    row_gain = mlp_gain.reshape(1, width)
    row_final = final_gain.reshape(1, width)

    rows = samples * PAD
    padding = pltpu.VMEM((PAD, width), F32)
    (normed_own,) = call(
        norm_kernel, (shape(rows, width, BF),), text_states, row_gain, scratch=[padding]
    )
    normed_far = move_txt(normed_own, z_hi=1)
    half = rows // 2

    valid_own = (jnp.arange(samples) < sample_count[0]).astype(BF)
    extra = jnp.stack([valid_own, text_length.astype(BF)], axis=1)
    image_rows = jnp.concatenate([image_pooled, jnp.pad(extra, ((0, 0), (0, 126)))], axis=1)
    image_rows = gather_txt(after(image_rows, normed_own))

    def ring_x(piece, *events):
        from_left = move_txt(piece, x=1)
        from_right = move_txt(piece, x=-1)
        relay_left, relay_right = from_left[:half], from_right[half:]
        if events:
            relay_left, relay_right = after(relay_left, *events), after(relay_right, *events)
        return piece, from_left, from_right, move_txt(relay_left, x=1), move_txt(relay_right, x=-1)

    pieces = ring_x(normed_own)
    pieces = (after(pieces[0], image_rows),) + pieces[1:]
    normed_near, act_near, slope_near, *terms_near = forward(pieces, up_weight, down_weight)
    image_rows = gather_z(image_rows)
    pieces = ring_x(normed_far)
    pieces = (after(pieces[0], image_rows),) + pieces[1:]
    normed_away, act_away, slope_away, *terms_away = forward(pieces, up_weight, down_weight)
    image_rows = gather_y(image_rows)
    away_left, away_right = ring_sum_start(terms_away)
    near_left, near_right = ring_sum_start(terms_near)
    away = (terms_away[0] + away_left.astype(F32) + away_right.astype(F32)).astype(BF)
    from_away = move_txt(after(away, image_rows), z_hi=1)

    image_all = gather_core(image_rows)
    valid = image_all[:, image_width] > 0.5
    lengths = image_all[: 8 * samples, image_width + 1].astype(jnp.int32)
    image_centred = centre(image_all[:, :image_width].astype(F32))
    image_normed = (image_centred * inv_std_of(image_centred) * image_gain).astype(BF)
    image_raw = jnp.dot(image_normed, image_proj, preferred_element_type=F32)
    image_unit, image_inv = unit_rows(image_raw)
    image_send = image_unit.astype(BF)

    pooled, hidden = call(
        final_kernel,
        (shape(samples, width, BF), shape(rows, width, BF)),
        text_length,
        text_states,
        terms_near[0],
        near_left,
        near_right,
        after(from_away, image_send),
        row_final,
        scratch=[padding],
        smem=1,
    )
    pooled_txt = gather_txt(pooled)
    hidden_far = move_txt(hidden, z_hi=1)
    pooled_z = gather_z(pooled_txt)
    pooled_y = gather_y(pooled_z)
    pooled_all = gather_core(pooled_y)
    hidden_near = ring_x(hidden, pooled_y)
    hidden_away = ring_x(after(hidden_far, pooled_y), pooled_all)

    text_raw = jnp.dot(pooled_all, text_proj, preferred_element_type=F32)
    text_unit, text_inv = unit_rows(text_raw)
    text_send = text_unit.astype(BF)
    scores = logit_scale * lax.dot_general(
        image_send, text_send, (((1,), (1,)), ((), ())), preferred_element_type=F32
    )
    batch = scores.shape[0]

    def masked_logsum(axis, mask):
        top = jnp.max(jnp.where(mask, scores, -1e30), axis=axis, keepdims=True)
        total = jnp.sum(jnp.exp(jnp.where(mask, scores - top, -1e30)), axis=axis, keepdims=True)
        return top + jnp.log(total)

    row_lse = masked_logsum(1, valid[None, :])
    col_lse = masked_logsum(0, valid[:, None])
    pair_mask = valid[:, None] & valid[None, :]
    row_prob = jnp.exp(jnp.where(pair_mask, scores - row_lse, -1e30))
    col_prob = jnp.exp(jnp.where(pair_mask, scores - col_lse, -1e30))
    same = jnp.arange(batch)[:, None] == jnp.arange(batch)[None, :]
    grad_scores = 0.5 * (row_prob + col_prob) - jnp.where(pair_mask & same, 1.0, 0.0)
    grad_high = lax.reduce_precision(grad_scores, 8, 7)
    grad_low = (grad_scores - grad_high).astype(BF)
    grad_high = grad_high.astype(BF)

    group = 8 * samples
    grad_text_unit = logit_scale * (
        lax.dot_general(grad_high[:, :group], image_send, OVER_ROWS, preferred_element_type=F32)
        + lax.dot_general(grad_low[:, :group], image_send, OVER_ROWS, preferred_element_type=F32)
    )
    grad_text_raw = unit_back(grad_text_unit, text_unit[:group], text_inv[:group]).astype(BF)
    grad_pooled = lax.dot_general(
        grad_text_raw, text_proj, (((1,), (1,)), ((), ())), preferred_element_type=F32
    )
    pulled = grad_pooled * final_gain
    core_at, y_at, z_at = (v.reshape(1).astype(jnp.int32) for v in (core, y, z_lo))
    units = act_near.shape[1]
    tokens = group * PAD
    sums = (shape(width // 2, units, BF), shape(width // 2, units, F32))
    grad_hidden, down_send, down_keep = call(
        hidden_kernel,
        (shape(tokens, width, BF),) + sums,
        core_at,
        lengths,
        *hidden_near,
        *hidden_away,
        pulled,
        act_near,
        act_away,
        smem=2,
        flops=2 * tokens * width * units,
    )
    up_send, up_keep = call(
        weights_kernel,
        sums,
        core_at,
        grad_hidden,
        down_weight,
        slope_near,
        slope_away,
        normed_near,
        normed_away,
        scratch=[pltpu.VMEM((tokens, units), BF)],
        smem=1,
        flops=4 * tokens * width * units,
    )
    down_grad = sum_img(down_send, down_keep, z_at, y_at).T
    up_grad = sum_img(up_send, up_keep, z_at, y_at)

    grad_high, grad_low = after(grad_high, up_send), after(grad_low, up_send)
    grad_image_unit = logit_scale * (
        jnp.dot(grad_high, text_send, preferred_element_type=F32)
        + jnp.dot(grad_low, text_send, preferred_element_type=F32)
    )
    grad_image_raw = unit_back(grad_image_unit, image_unit, image_inv).astype(BF)
    columns = grad_image_raw.shape[1] // 32
    chosen = jnp.arange(grad_image_raw.shape[1])[:, None] == (
        img * columns + jnp.arange(columns)[None, :]
    )
    own_columns = jnp.dot(
        grad_image_raw, chosen.astype(BF), preferred_element_type=F32
    ).astype(BF)
    projected = lax.dot_general(image_normed, own_columns, OVER_ROWS, preferred_element_type=F32)
    rows = image_width // 8
    image_proj_grad = lax.dynamic_slice_in_dim(projected, txt * rows, rows, axis=0)
    return (image_proj_grad, up_grad, down_grad)


def solution(mesh):
    return jax.shard_map(
        body,
        mesh=mesh,
        in_specs=(
            P(("img", "txt"), None, None),
            P(("img", "txt")),
            P(("img", "txt")),
            P(),
            P(None, "txt"),
            P("txt", None),
            P(),
            P(),
            P(("img", "txt"), None),
            P(),
            P(),
            P(),
        ),
        out_specs=(P("txt", "img"), P("img", "txt"), P("txt", "img")),
        check_vma=False,
    )
```

```python
import jax
import jax.numpy as jnp
from jax import lax
from jax.experimental import pallas as pl
from jax.experimental.pallas import tpu as pltpu
from jax.sharding import PartitionSpec as P

EPSILON = 1e-05
ROOT_HALF = 0.7071067811865476
INV_ROOT_TAU = 0.3989422804014327
BF = jnp.bfloat16
F32 = jnp.float32
PAD = 80


def centre(values):
    return values - jnp.mean(values, axis=-1, keepdims=True)


def inv_std_of(centred):
    return lax.rsqrt(jnp.mean(centred * centred, axis=-1, keepdims=True) + EPSILON)


def unit_rows(raw):
    inv_norm = lax.rsqrt(jnp.sum(raw * raw, axis=-1, keepdims=True) + 1e-06)
    return (raw * inv_norm, inv_norm)


def unit_back(grad_unit, direction, inv_norm):
    return inv_norm * (
        grad_unit - direction * jnp.sum(direction * grad_unit, axis=-1, keepdims=True)
    )


VMEM_LIMIT = 40 * 1024 * 1024
OVER_ROWS = (((0,), (0,)), ((), ()))
OVER_COLS = (((1,), (1,)), ((), ()))


def call(kernel, outs, *operands, scratch=(), smem=0, flops=0):
    size = sum(v.size * v.dtype.itemsize for v in operands) + sum(
        v.size * v.dtype.itemsize for v in outs
    )
    specs = [pl.BlockSpec(memory_space=pltpu.SMEM)] * smem
    specs += [pl.BlockSpec(memory_space=pltpu.VMEM)] * (len(operands) - smem)
    return pl.pallas_call(
        kernel,
        out_shape=outs,
        in_specs=specs,
        out_specs=[pl.BlockSpec(memory_space=pltpu.VMEM)] * len(outs),
        scratch_shapes=list(scratch),
        cost_estimate=pl.CostEstimate(flops=flops, bytes_accessed=size, transcendentals=0),
        compiler_params=pltpu.CompilerParams(vmem_limit_bytes=VMEM_LIMIT),
    )(*operands)


def shape(rows, cols, dtype):
    return jax.ShapeDtypeStruct((rows, cols), dtype)


def padded(states_ref, slot, scratch):
    length = states_ref.shape[1]
    scratch[PAD - 8 :, :] = jnp.zeros((8, scratch.shape[1]), F32)
    scratch[:length, :] = states_ref[slot].astype(F32)
    return scratch[...]


def norm_kernel(states_ref, gain_ref, out_ref, scratch):
    for slot in range(states_ref.shape[0]):
        centred = centre(padded(states_ref, slot, scratch))
        scaled = centred * inv_std_of(centred) * gain_ref[...]
        out_ref[slot * PAD : (slot + 1) * PAD, :] = scaled.astype(BF)


def forward_kernel(normed_ref, up_ref, down_ref, act_ref, slope_ref, out_ref):
    half = normed_ref.shape[0] // 2
    for part in range(2):
        span = slice(part * half, (part + 1) * half)
        preact = jnp.dot(normed_ref[span, :], up_ref[...], preferred_element_type=F32)
        cdf = 0.5 * (1.0 + lax.erf(preact * ROOT_HALF))
        act_ref[span, :] = (preact * cdf).astype(BF)
        slope = cdf + preact * INV_ROOT_TAU * jnp.exp(-0.5 * preact * preact)
        slope_ref[span, :] = slope.astype(BF)
        out = jnp.dot(act_ref[span, :], down_ref[...], preferred_element_type=F32)
        out_ref[span, :] = out.astype(BF)


def away_kernel(terms_ref, out_ref):
    rows = out_ref.shape[0]
    total = terms_ref[:rows, :].astype(F32)
    for k in range(1, 4):
        total = total + terms_ref[k * rows : (k + 1) * rows, :].astype(F32)
    out_ref[...] = total.astype(BF)


def final_kernel(
    length_ref, states_ref, near_ref, away_ref, gain_ref,
    pooled_ref, centred_ref, scratch,
):
    pooled = []
    for slot in range(states_ref.shape[0]):
        span = slice(slot * PAD, (slot + 1) * PAD)
        total = away_ref[span, :].astype(F32)
        for k in range(4):
            place = k * away_ref.shape[0] + slot * PAD
            total = total + near_ref[place : place + PAD, :].astype(F32)
        centred = centre(padded(states_ref, slot, scratch) + total)
        centred_ref[span, :] = centred.astype(BF)
        count = length_ref[slot]
        kept = (lax.broadcasted_iota(jnp.int32, (PAD, 1), 0) < count).astype(F32)
        weight = kept * inv_std_of(centred) / count.astype(F32)
        pooled.append(jnp.sum(centred * weight, axis=0, keepdims=True) * gain_ref[...])
    pooled_ref[...] = jnp.concatenate(pooled, axis=0).astype(BF)


def split_core(core, rows, part, send_ref, keep_ref):
    run = 40
    for j in range(rows.shape[0] // (4 * run)):
        first = rows[j * 4 * run : j * 4 * run + run]
        second = rows[j * 4 * run + run : j * 4 * run + 2 * run]
        third = rows[j * 4 * run + 2 * run : j * 4 * run + 3 * run]
        fourth = rows[j * 4 * run + 3 * run : j * 4 * run + 4 * run]
        even = jnp.concatenate([first, third], axis=0)
        odd = jnp.concatenate([second, fourth], axis=0)
        base = part * rows.shape[0] // 2 + j * 2 * run
        span = slice(base, base + 2 * run)
        send_ref[span, :] = jnp.where(core == 0, odd, even).astype(BF)
        keep_ref[span, :] = jnp.where(core == 0, even, odd)


def hidden_kernel(
    core_ref, length_ref, order_ref, near_ref, far_ref, pulled_ref, act_a_ref, act_b_ref,
    grad_ref, send_ref, keep_ref,
):
    place = 0
    for ref in (near_ref, far_ref):
        grad_ref[place : place + ref.shape[0], :] = ref[...]
        place += ref.shape[0]

    def sample(index, carry):
        span = pl.ds(pl.multiple_of(index * PAD, PAD), PAD)
        centred = grad_ref[span, :].astype(F32)
        inv = inv_std_of(centred)
        hat = centred * inv
        source = order_ref[index]
        pulled = pulled_ref[pl.ds(source, 1), :]
        along = jnp.mean(pulled * hat, axis=-1, keepdims=True)
        count = length_ref[source]
        kept = (lax.broadcasted_iota(jnp.int32, (PAD, 1), 0) < count).astype(F32)
        weight = kept * inv / count.astype(F32)
        grad = weight * (pulled - jnp.mean(pulled, axis=-1, keepdims=True) - hat * along)
        grad_ref[span, :] = grad.astype(BF)
        return carry

    lax.fori_loop(0, place // PAD, sample, 0)
    tokens = act_a_ref.shape[0]
    for part in range(2):
        cols = slice(part * 640, (part + 1) * 640)
        rows = lax.dot_general(
            grad_ref[:tokens, cols], act_a_ref[...], OVER_ROWS, preferred_element_type=F32
        ) + lax.dot_general(
            grad_ref[tokens:, cols], act_b_ref[...], OVER_ROWS, preferred_element_type=F32
        )
        split_core(core_ref[0], rows, part, send_ref, keep_ref)


def weights_kernel(
    core_ref, grad_ref, down_ref, slope_a_ref, slope_b_ref, normed_a_ref, normed_b_ref,
    send_ref, keep_ref, scratch,
):
    tokens = slope_a_ref.shape[0]
    for part, slope_ref in enumerate((slope_a_ref, slope_b_ref)):
        span = slice(part * tokens, (part + 1) * tokens)
        back = lax.dot_general(
            grad_ref[span, :], down_ref[...], OVER_COLS, preferred_element_type=F32
        )
        scratch[span, :] = (back * slope_ref[...].astype(F32)).astype(BF)
    for part in range(2):
        cols = slice(part * 640, (part + 1) * 640)
        rows = lax.dot_general(
            normed_a_ref[:, cols], scratch[:tokens, :], OVER_ROWS, preferred_element_type=F32
        ) + lax.dot_general(
            normed_b_ref[:, cols], scratch[tokens:, :], OVER_ROWS, preferred_element_type=F32
        )
        split_core(core_ref[0], rows, part, send_ref, keep_ref)


def move_txt(value, z_hi=0, x=0):
    pairs = [
        (a * 4 + b, ((a + z_hi) % 2) * 4 + (b + x) % 4) for a in range(2) for b in range(4)
    ]
    return lax.ppermute(value, "txt", pairs)


def move_img(value, z_lo=0, y=0, core=0):
    pairs = [
        (a * 8 + b * 2 + c, ((a + z_lo) % 4) * 8 + ((b + y) % 4) * 2 + (c + core) % 2)
        for a in range(4)
        for b in range(4)
        for c in range(2)
    ]
    return lax.ppermute(value, "img", pairs)


def after(value, *events):
    return lax.optimization_barrier((value,) + events)[0]


def swap(blocks, axis, groups):
    return lax.all_to_all(blocks, axis, 0, 0, axis_index_groups=groups)


def gather(rows, axis, groups):
    count = len(groups[0])
    got = swap(jnp.broadcast_to(rows[None], (count,) + rows.shape), axis, groups)
    return got.reshape(count * rows.shape[0], rows.shape[1])


def pick(value, index, axis):
    return lax.dynamic_index_in_dim(value, index, axis, keepdims=False)


BOTH = ("img", "txt")
ALONG_X = [[a * 4 + b for b in range(4)] for a in range(2)]
SAME_CORE = [[a * 8 + b * 2 + c for a in range(4) for b in range(4)] for c in range(2)]
SAME_CORE_X = [
    [(a * 8 + b * 2 + c) * 8 + z * 4 + x for a in range(4) for b in range(4) for z in range(2)]
    for c in range(2)
    for x in range(4)
]
ALL_CORE = [
    [(a * 8 + b * 2 + c) * 8 + t for a in range(4) for b in range(4) for t in range(8)]
    for c in range(2)
]


def forward(normed, up_weight, down_weight):
    tokens = normed.shape[0]
    width, units = up_weight.shape
    return call(
        forward_kernel,
        (shape(tokens, units, BF), shape(tokens, units, BF), shape(tokens, width, BF)),
        normed,
        up_weight,
        down_weight,
        flops=4 * tokens * width * units,
    )


def sum_img(send, keep):
    got = move_img(send, core=1)
    blocks = (keep + got.astype(F32)).astype(BF).reshape(16, 40, keep.shape[1])
    return jnp.sum(swap(blocks, "img", SAME_CORE).astype(F32), axis=0)


def body(
    text_states,
    text_length,
    sample_count,
    mlp_gain,
    up_weight,
    down_weight,
    final_gain,
    text_proj,
    image_pooled,
    image_gain,
    image_proj,
    logit_scale,
):
    samples, length, width = text_states.shape
    image_width = image_pooled.shape[1]
    txt = lax.axis_index("txt")
    img = lax.axis_index("img")
    z_lo, y, core = img // 8, (img // 2) % 4, img % 2

    row_gain = mlp_gain.reshape(1, width)
    row_final = final_gain.reshape(1, width)

    rows = samples * PAD
    padding = pltpu.VMEM((PAD, width), F32)
    (normed_own,) = call(
        norm_kernel, (shape(rows, width, BF),), text_states, row_gain, scratch=[padding]
    )
    normed_far = move_txt(normed_own, z_hi=1)

    valid_own = (jnp.arange(samples) < sample_count[0]).astype(BF)
    extra = jnp.stack([valid_own, text_length.astype(BF)], axis=1)
    image_rows = jnp.concatenate([image_pooled, jnp.pad(extra, ((0, 0), (0, 126)))], axis=1)

    def from_x(piece):
        return gather(piece, "txt", ALONG_X)

    def to_x(terms):
        return swap(terms.reshape(4, rows, width), "txt", ALONG_X).reshape(4 * rows, width)

    normed_near = from_x(normed_own)
    image_rows = gather(after(image_rows, normed_near), "txt", ALONG_X)
    image_rows = gather(image_rows, BOTH, SAME_CORE_X)
    act_near, slope_near, terms_near = forward(normed_near, up_weight, down_weight)
    normed_away = from_x(normed_far)
    act_away, slope_away, terms_away = forward(normed_away, up_weight, down_weight)
    terms_away = to_x(terms_away)
    terms_near = to_x(terms_near)
    (away,) = call(away_kernel, (shape(rows, width, BF),), terms_away)
    from_away = move_txt(away, z_hi=1)

    group = 8 * samples
    place = (z_lo * 4 + y) * group
    image_rows = after(image_rows, act_away)
    image_all = jnp.concatenate([image_rows, move_img(image_rows, core=1)], axis=0)
    valid = image_all[:, image_width] > 0.5
    lengths = lax.dynamic_slice_in_dim(image_all[:, image_width + 1], place, group)
    lengths = lengths.astype(jnp.int32)
    image_centred = centre(image_all[:, :image_width].astype(F32))
    image_normed = (image_centred * inv_std_of(image_centred) * image_gain).astype(BF)
    image_raw = jnp.dot(image_normed, image_proj, preferred_element_type=F32)
    image_unit, image_inv = unit_rows(image_raw)
    image_send = image_unit.astype(BF)

    pooled, hidden = call(
        final_kernel,
        (shape(samples, width, BF), shape(rows, width, BF)),
        text_length,
        text_states,
        terms_near,
        after(from_away, image_send),
        row_final,
        scratch=[padding],
        smem=1,
    )
    hidden_far = move_txt(hidden, z_hi=1)
    pooled_all = gather(pooled, BOTH, ALL_CORE)
    hidden_near = from_x(hidden)
    pooled_all = jnp.concatenate([pooled_all, move_img(pooled_all, core=1)], axis=0)
    hidden_away = from_x(hidden_far)

    text_raw = jnp.dot(pooled_all, text_proj, preferred_element_type=F32)
    text_unit, text_inv = unit_rows(text_raw)
    text_send = text_unit.astype(BF)
    scores = logit_scale * lax.dot_general(
        text_send, image_send, OVER_COLS, preferred_element_type=F32
    )
    batch = scores.shape[0]

    def masked_logsum(axis, mask):
        top = jnp.max(jnp.where(mask, scores, -1e30), axis=axis, keepdims=True)
        total = jnp.sum(jnp.exp(jnp.where(mask, scores - top, -1e30)), axis=axis, keepdims=True)
        return top + jnp.log(total)

    row_lse = masked_logsum(0, valid[:, None])
    col_lse = masked_logsum(1, valid[None, :])
    pair_mask = valid[:, None] & valid[None, :]
    row_prob = jnp.exp(jnp.where(pair_mask, scores - row_lse, -1e30))
    col_prob = jnp.exp(jnp.where(pair_mask, scores - col_lse, -1e30))
    same = jnp.arange(batch)[:, None] == jnp.arange(batch)[None, :]
    grad_scores = 0.5 * (row_prob + col_prob) - jnp.where(pair_mask & same, 1.0, 0.0)
    grad_high = lax.reduce_precision(grad_scores, 8, 7)
    grad_low = (grad_scores - grad_high).astype(BF)
    grad_high = grad_high.astype(BF)

    def own(value):
        return lax.dynamic_slice_in_dim(value, place, group, axis=0)

    grad_text_unit = logit_scale * (
        jnp.dot(own(grad_high), image_send, preferred_element_type=F32)
        + jnp.dot(own(grad_low), image_send, preferred_element_type=F32)
    )
    grad_text_raw = unit_back(grad_text_unit, own(text_unit), own(text_inv)).astype(BF)
    grad_pooled = lax.dot_general(
        grad_text_raw, text_proj, OVER_COLS, preferred_element_type=F32
    )
    pulled = grad_pooled * final_gain
    order = ((txt // 4 + jnp.arange(2)) % 2)[:, None] * (group // 2) + jnp.arange(group // 2)
    order = order.reshape(group).astype(jnp.int32)
    core_at = core.reshape(1).astype(jnp.int32)
    units = act_near.shape[1]
    tokens = group * PAD
    sums = (shape(width // 2, units, BF), shape(width // 2, units, F32))
    grad_hidden, down_send, down_keep = call(
        hidden_kernel,
        (shape(tokens, width, BF),) + sums,
        core_at,
        lengths,
        order,
        hidden_near,
        hidden_away,
        pulled,
        act_near,
        act_away,
        smem=3,
        flops=2 * tokens * width * units,
    )
    up_send, up_keep = call(
        weights_kernel,
        sums,
        core_at,
        grad_hidden,
        down_weight,
        slope_near,
        slope_away,
        normed_near,
        normed_away,
        scratch=[pltpu.VMEM((tokens, units), BF)],
        smem=1,
        flops=4 * tokens * width * units,
    )
    down_grad = sum_img(down_send, down_keep).T
    up_grad = sum_img(up_send, up_keep)

    grad_high, grad_low = after(grad_high, up_send), after(grad_low, up_send)
    grad_image_unit = logit_scale * (
        lax.dot_general(grad_high, text_send, OVER_ROWS, preferred_element_type=F32)
        + lax.dot_general(grad_low, text_send, OVER_ROWS, preferred_element_type=F32)
    )
    grad_image_raw = unit_back(grad_image_unit, image_unit, image_inv).astype(BF)
    columns = grad_image_raw.shape[1] // 32
    chosen = jnp.arange(grad_image_raw.shape[1])[:, None] == (
        img * columns + jnp.arange(columns)[None, :]
    )
    own_columns = jnp.dot(
        grad_image_raw, chosen.astype(BF), preferred_element_type=F32
    ).astype(BF)
    projected = lax.dot_general(image_normed, own_columns, OVER_ROWS, preferred_element_type=F32)
    rows = image_width // 8
    image_proj_grad = lax.dynamic_slice_in_dim(projected, txt * rows, rows, axis=0)
    return (image_proj_grad, up_grad, down_grad)


def solution(mesh):
    return jax.shard_map(
        body,
        mesh=mesh,
        in_specs=(
            P(("img", "txt"), None, None),
            P(("img", "txt")),
            P(("img", "txt")),
            P(),
            P(None, "txt"),
            P("txt", None),
            P(),
            P(),
            P(("img", "txt"), None),
            P(),
            P(),
            P(),
        ),
        out_specs=(P("txt", "img"), P("img", "txt"), P("txt", "img")),
        check_vma=False,
    )
```

```python
import jax
import jax.numpy as jnp
from jax import lax
from jax.experimental import pallas as pl
from jax.experimental.pallas import tpu as pltpu
from jax.sharding import PartitionSpec as P

EPSILON = 1e-05
ROOT_HALF = 0.7071067811865476
INV_ROOT_TAU = 0.3989422804014327
BF = jnp.bfloat16
F32 = jnp.float32
PAD = 80


def centre(values):
    return values - jnp.mean(values, axis=-1, keepdims=True)


def inv_std_of(centred):
    return lax.rsqrt(jnp.mean(centred * centred, axis=-1, keepdims=True) + EPSILON)


def unit_rows(raw):
    inv_norm = lax.rsqrt(jnp.sum(raw * raw, axis=-1, keepdims=True) + 1e-06)
    return (raw * inv_norm, inv_norm)


def unit_back(grad_unit, direction, inv_norm):
    return inv_norm * (
        grad_unit - direction * jnp.sum(direction * grad_unit, axis=-1, keepdims=True)
    )


VMEM_LIMIT = 40 * 1024 * 1024
OVER_ROWS = (((0,), (0,)), ((), ()))
OVER_COLS = (((1,), (1,)), ((), ()))


def call(kernel, outs, *operands, scratch=(), smem=0, flops=0):
    size = sum(v.size * v.dtype.itemsize for v in operands) + sum(
        v.size * v.dtype.itemsize for v in outs
    )
    specs = [pl.BlockSpec(memory_space=pltpu.SMEM)] * smem
    specs += [pl.BlockSpec(memory_space=pltpu.VMEM)] * (len(operands) - smem)
    return pl.pallas_call(
        kernel,
        out_shape=outs,
        in_specs=specs,
        out_specs=[pl.BlockSpec(memory_space=pltpu.VMEM)] * len(outs),
        scratch_shapes=list(scratch),
        cost_estimate=pl.CostEstimate(flops=flops, bytes_accessed=size, transcendentals=0),
        compiler_params=pltpu.CompilerParams(vmem_limit_bytes=VMEM_LIMIT),
    )(*operands)


def shape(rows, cols, dtype):
    return jax.ShapeDtypeStruct((rows, cols), dtype)


def padded(states_ref, slot, scratch):
    length = states_ref.shape[1]
    scratch[PAD - 8 :, :] = jnp.zeros((8, scratch.shape[1]), F32)
    scratch[:length, :] = states_ref[slot].astype(F32)
    return scratch[...]


def norm_kernel(states_ref, gain_ref, out_ref, scratch):
    for slot in range(states_ref.shape[0]):
        centred = centre(padded(states_ref, slot, scratch))
        scaled = centred * inv_std_of(centred) * gain_ref[...]
        out_ref[slot * PAD : (slot + 1) * PAD, :] = scaled.astype(BF)


def forward_kernel(
    own_ref, left_ref, right_ref, far_ref, up_ref, down_ref,
    normed_ref, act_ref, slope_ref, o_own, o_left, o_right, o_far,
):
    rows = own_ref.shape[0]
    for k, ref in enumerate((own_ref, left_ref, right_ref, far_ref)):
        normed_ref[k * rows : (k + 1) * rows, :] = ref[...]
    for part, (first, second) in enumerate(((o_own, o_left), (o_right, o_far))):
        span = slice(2 * part * rows, 2 * (part + 1) * rows)
        preact = jnp.dot(normed_ref[span, :], up_ref[...], preferred_element_type=F32)
        cdf = 0.5 * (1.0 + lax.erf(preact * ROOT_HALF))
        act_ref[span, :] = (preact * cdf).astype(BF)
        slope = cdf + preact * INV_ROOT_TAU * jnp.exp(-0.5 * preact * preact)
        slope_ref[span, :] = slope.astype(BF)
        out = jnp.dot(act_ref[span, :], down_ref[...], preferred_element_type=F32)
        first[...] = out[:rows].astype(first.dtype)
        second[...] = out[rows:].astype(second.dtype)


def away_kernel(own_ref, left_ref, right_ref, far_ref, out_ref):
    total = own_ref[...] + left_ref[...].astype(F32) + right_ref[...].astype(F32)
    out_ref[...] = (total + far_ref[...].astype(F32)).astype(BF)


def final_kernel(
    length_ref, states_ref, own_ref, left_ref, right_ref, far_ref, away_ref, gain_ref,
    pooled_ref, centred_ref, scratch,
):
    pooled = []
    for slot in range(states_ref.shape[0]):
        span = slice(slot * PAD, (slot + 1) * PAD)
        total = own_ref[span, :] + left_ref[span, :].astype(F32) + right_ref[span, :].astype(F32)
        total = total + far_ref[span, :].astype(F32) + away_ref[span, :].astype(F32)
        centred = centre(padded(states_ref, slot, scratch) + total)
        centred_ref[span, :] = centred.astype(BF)
        count = length_ref[slot]
        kept = (lax.broadcasted_iota(jnp.int32, (PAD, 1), 0) < count).astype(F32)
        weight = kept * inv_std_of(centred) / count.astype(F32)
        pooled.append(jnp.sum(centred * weight, axis=0, keepdims=True) * gain_ref[...])
    pooled_ref[...] = jnp.concatenate(pooled, axis=0).astype(BF)


def split_core(core, rows, part, send_ref, keep_ref):
    run = 40
    for j in range(rows.shape[0] // (4 * run)):
        first = rows[j * 4 * run : j * 4 * run + run]
        second = rows[j * 4 * run + run : j * 4 * run + 2 * run]
        third = rows[j * 4 * run + 2 * run : j * 4 * run + 3 * run]
        fourth = rows[j * 4 * run + 3 * run : j * 4 * run + 4 * run]
        even = jnp.concatenate([first, third], axis=0)
        odd = jnp.concatenate([second, fourth], axis=0)
        base = part * rows.shape[0] // 2 + j * 2 * run
        span = slice(base, base + 2 * run)
        send_ref[span, :] = jnp.where(core == 0, odd, even).astype(BF)
        keep_ref[span, :] = jnp.where(core == 0, even, odd)


def hidden_kernel(
    core_ref, length_ref, h0, h1, h2, h3, h4, h5, h6, h7, pulled_ref, act_a_ref, act_b_ref,
    grad_ref, send_ref, keep_ref,
):
    place = 0
    for ref in (h0, h1, h2, h3, h4, h5, h6, h7):
        grad_ref[place : place + ref.shape[0], :] = ref[...]
        place += ref.shape[0]

    def sample(index, carry):
        span = pl.ds(pl.multiple_of(index * PAD, PAD), PAD)
        centred = grad_ref[span, :].astype(F32)
        inv = inv_std_of(centred)
        hat = centred * inv
        pulled = pulled_ref[pl.ds(index, 1), :]
        along = jnp.mean(pulled * hat, axis=-1, keepdims=True)
        count = length_ref[index]
        kept = (lax.broadcasted_iota(jnp.int32, (PAD, 1), 0) < count).astype(F32)
        weight = kept * inv / count.astype(F32)
        grad = weight * (pulled - jnp.mean(pulled, axis=-1, keepdims=True) - hat * along)
        grad_ref[span, :] = grad.astype(BF)
        return carry

    lax.fori_loop(0, place // PAD, sample, 0)
    tokens = act_a_ref.shape[0]
    for part in range(2):
        cols = slice(part * 640, (part + 1) * 640)
        rows = lax.dot_general(
            grad_ref[:tokens, cols], act_a_ref[...], OVER_ROWS, preferred_element_type=F32
        ) + lax.dot_general(
            grad_ref[tokens:, cols], act_b_ref[...], OVER_ROWS, preferred_element_type=F32
        )
        split_core(core_ref[0], rows, part, send_ref, keep_ref)


def weights_kernel(
    core_ref, grad_ref, down_ref, slope_a_ref, slope_b_ref, normed_a_ref, normed_b_ref,
    send_ref, keep_ref, scratch,
):
    tokens = slope_a_ref.shape[0]
    for part, slope_ref in enumerate((slope_a_ref, slope_b_ref)):
        span = slice(part * tokens, (part + 1) * tokens)
        back = lax.dot_general(
            grad_ref[span, :], down_ref[...], OVER_COLS, preferred_element_type=F32
        )
        scratch[span, :] = (back * slope_ref[...].astype(F32)).astype(BF)
    for part in range(2):
        cols = slice(part * 640, (part + 1) * 640)
        rows = lax.dot_general(
            normed_a_ref[:, cols], scratch[:tokens, :], OVER_ROWS, preferred_element_type=F32
        ) + lax.dot_general(
            normed_b_ref[:, cols], scratch[tokens:, :], OVER_ROWS, preferred_element_type=F32
        )
        split_core(core_ref[0], rows, part, send_ref, keep_ref)


def spread_y_kernel(y_ref, keep_ref, got_ref, own_ref, s1_ref, s2_ref, s3_ref, scratch):
    scratch[...] = keep_ref[...] + got_ref[...].astype(F32)
    for shift, ref in ((0, own_ref), (1, s1_ref), (3, s2_ref), (2, s3_ref)):
        place = lax.rem(y_ref[0] + shift, 4) * 40
        for pair in range(2):
            runs = [
                scratch[pl.ds(pl.multiple_of((2 * pair + k) * 160 + place, 8), 40), :]
                for k in range(2)
            ]
            ref[pair * 80 : (pair + 1) * 80, :] = jnp.concatenate(runs, axis=0).astype(ref.dtype)


def spread_z_kernel(z_ref, keep_ref, r1_ref, r2_ref, r3_ref, own_ref, s1_ref, s2_ref, s3_ref, scratch):
    scratch[...] = (
        keep_ref[...]
        + r1_ref[...].astype(F32)
        + r2_ref[...].astype(F32)
        + r3_ref[...].astype(F32)
    )
    for shift, ref in ((0, own_ref), (1, s1_ref), (3, s2_ref), (2, s3_ref)):
        place = lax.rem(z_ref[0] + shift, 4) * 40
        ref[...] = scratch[pl.ds(pl.multiple_of(place, 8), 40), :].astype(ref.dtype)


def move_txt(value, z_hi=0, x=0):
    pairs = [
        (a * 4 + b, ((a + z_hi) % 2) * 4 + (b + x) % 4) for a in range(2) for b in range(4)
    ]
    return lax.ppermute(value, "txt", pairs)


def move_img(value, z_lo=0, y=0, core=0):
    pairs = [
        (a * 8 + b * 2 + c, ((a + z_lo) % 4) * 8 + ((b + y) % 4) * 2 + (c + core) % 2)
        for a in range(4)
        for b in range(4)
        for c in range(2)
    ]
    return lax.ppermute(value, "img", pairs)


def after(value, *events):
    return lax.optimization_barrier((value,) + events)[0]


def move_z(value, shift):
    pairs = []
    for z in range(8):
        to = (z + shift) % 8
        for rest in range(8):
            for x in range(4):
                pairs.append(
                    (((z % 4) * 8 + rest) * 8 + (z // 4) * 4 + x, ((to % 4) * 8 + rest) * 8 + (to // 4) * 4 + x)
                )
    return lax.ppermute(value, ("img", "txt"), pairs)


def joined(*rows):
    return lax.optimization_barrier(jnp.concatenate(rows, axis=0))


def gather_x(rows):
    return joined(rows, move_txt(rows, x=1), move_txt(rows, x=-1), move_txt(rows, x=2))


def gather_z(rows):
    return joined(rows, move_z(rows, 1), move_z(rows, -1))


def gather_far_z(rows):
    return joined(rows, move_z(rows, 3), move_z(rows[: rows.shape[0] // 3 * 2], -3))


def gather_y(rows):
    return joined(rows, move_img(rows, y=1), move_img(rows, y=-1), move_img(rows, y=2))


def gather_core(rows):
    return jnp.concatenate([rows, move_img(rows, core=1)], axis=0)


def group_rows(rows):
    return jnp.concatenate([rows[:8], rows[32:40]], axis=0)


def ring_x(piece):
    return piece, move_txt(piece, x=1), move_txt(piece, x=-1), move_txt(piece, x=2)


def ring_x_back(terms):
    own, left, right, far = terms
    return own, move_txt(left, x=-1), move_txt(right, x=1), move_txt(far, x=2)


def forward(pieces, up_weight, down_weight):
    rows = pieces[0].shape[0]
    tokens = 4 * rows
    width, units = up_weight.shape
    return call(
        forward_kernel,
        (
            shape(tokens, width, BF),
            shape(tokens, units, BF),
            shape(tokens, units, BF),
            shape(rows, width, F32),
        )
        + (shape(rows, width, BF),) * 3,
        *pieces,
        up_weight,
        down_weight,
        flops=4 * tokens * width * units,
    )


def sum_img_start(send, keep, y):
    got = move_img(send, core=1)
    cols = keep.shape[1]
    outs = (shape(160, cols, F32),) + (shape(160, cols, BF),) * 3
    own, s1, s2, s3 = call(
        spread_y_kernel, outs, y, keep, got, scratch=[pltpu.VMEM(keep.shape, F32)], smem=1
    )
    return own, s1, s2, s3


def sum_img_end(terms, z_lo):
    own, s1, s2, s3 = terms
    cols = own.shape[1]
    s3, s1, s2 = move_img(s3, y=2), move_img(s1, y=1), move_img(s2, y=-1)
    outs = (shape(40, cols, F32),) + (shape(40, cols, BF),) * 3
    own, s1, s2, s3 = call(
        spread_z_kernel, outs, z_lo, own, s1, s2, s3,
        scratch=[pltpu.VMEM((160, cols), F32)], smem=1,
    )
    s3, s1, s2 = move_img(s3, z_lo=2), move_img(s1, z_lo=1), move_img(s2, z_lo=-1)
    return own + s1.astype(F32) + s2.astype(F32) + s3.astype(F32)


def body(
    text_states,
    text_length,
    sample_count,
    mlp_gain,
    up_weight,
    down_weight,
    final_gain,
    text_proj,
    image_pooled,
    image_gain,
    image_proj,
    logit_scale,
):
    samples, length, width = text_states.shape
    image_width = image_pooled.shape[1]
    txt = lax.axis_index("txt")
    img = lax.axis_index("img")
    z_lo, y, core = img // 8, (img // 2) % 4, img % 2

    row_gain = mlp_gain.reshape(1, width)
    row_final = final_gain.reshape(1, width)

    rows = samples * PAD
    padding = pltpu.VMEM((PAD, width), F32)
    (normed_own,) = call(
        norm_kernel, (shape(rows, width, BF),), text_states, row_gain, scratch=[padding]
    )
    near = ring_x(normed_own)
    normed_far = after(move_txt(normed_own, z_hi=1), near[1])

    valid_own = (jnp.arange(samples) < sample_count[0]).astype(BF)
    extra = jnp.stack([valid_own, text_length.astype(BF)], axis=1)
    image_rows = jnp.concatenate([image_pooled, jnp.pad(extra, ((0, 0), (0, 126)))], axis=1)
    image_rows = gather_x(after(image_rows, near[1]))

    away = ring_x(normed_far)
    image_rows = gather_far_z(after(gather_z(image_rows), normed_far))
    normed_near, act_near, slope_near, *terms_near = forward(near, up_weight, down_weight)
    image_rows = gather_y(after(image_rows, act_near))
    normed_away, act_away, slope_away, *terms_away = forward(away, up_weight, down_weight)
    terms_away = ring_x_back(terms_away)
    terms_near = ring_x_back(terms_near)
    (away_sum,) = call(away_kernel, (shape(rows, width, BF),), *terms_away)
    from_away = move_txt(away_sum, z_hi=1)

    image_all = gather_core(after(image_rows, act_away))
    valid = image_all[:, image_width] > 0.5
    lengths = group_rows(image_all[:64])[:, image_width + 1].astype(jnp.int32)
    image_centred = centre(image_all[:, :image_width].astype(F32))
    image_normed = (image_centred * inv_std_of(image_centred) * image_gain).astype(BF)
    image_raw = jnp.dot(image_normed, image_proj, preferred_element_type=F32)
    image_unit, image_inv = unit_rows(image_raw)
    image_send = image_unit.astype(BF)

    pooled, hidden = call(
        final_kernel,
        (shape(samples, width, BF), shape(rows, width, BF)),
        text_length,
        text_states,
        *terms_near,
        after(from_away, image_send),
        row_final,
        scratch=[padding],
        smem=1,
    )
    pooled_x = gather_x(pooled)
    hidden_far = move_txt(hidden, z_hi=1)
    pooled_z = gather_far_z(gather_z(pooled_x))
    hidden_near = ring_x(after(hidden, pooled_x))
    pooled_all = gather_core(gather_y(pooled_z))
    hidden_away = ring_x(after(hidden_far, pooled_z))

    group = 8 * samples
    text_raw = jnp.dot(pooled_all, text_proj, preferred_element_type=F32)
    text_unit, text_inv = unit_rows(text_raw)
    text_send = text_unit.astype(BF)
    scores = logit_scale * lax.dot_general(
        text_send, image_send, OVER_COLS, preferred_element_type=F32
    )
    batch = scores.shape[0]

    def masked_logsum(axis, mask):
        top = jnp.max(jnp.where(mask, scores, -1e30), axis=axis, keepdims=True)
        total = jnp.sum(jnp.exp(jnp.where(mask, scores - top, -1e30)), axis=axis, keepdims=True)
        return top + jnp.log(total)

    row_lse = masked_logsum(0, valid[:, None])
    col_lse = masked_logsum(1, valid[None, :])
    pair_mask = valid[:, None] & valid[None, :]
    row_prob = jnp.exp(jnp.where(pair_mask, scores - row_lse, -1e30))
    col_prob = jnp.exp(jnp.where(pair_mask, scores - col_lse, -1e30))
    same = jnp.arange(batch)[:, None] == jnp.arange(batch)[None, :]
    grad_scores = 0.5 * (row_prob + col_prob) - jnp.where(pair_mask & same, 1.0, 0.0)
    grad_high = lax.reduce_precision(grad_scores, 8, 7)
    grad_low = (grad_scores - grad_high).astype(BF)
    grad_high = grad_high.astype(BF)

    grad_text_unit = logit_scale * (
        jnp.dot(group_rows(grad_high), image_send, preferred_element_type=F32)
        + jnp.dot(group_rows(grad_low), image_send, preferred_element_type=F32)
    )
    grad_text_raw = unit_back(grad_text_unit, group_rows(text_unit), group_rows(text_inv)).astype(BF)
    grad_pooled = lax.dot_general(
        grad_text_raw, text_proj, OVER_COLS, preferred_element_type=F32
    )
    pulled = grad_pooled * final_gain
    core_at, y_at, z_at = (v.reshape(1).astype(jnp.int32) for v in (core, y, z_lo))
    units = act_near.shape[1]
    tokens = group * PAD
    sums = (shape(width // 2, units, BF), shape(width // 2, units, F32))
    grad_hidden, down_send, down_keep = call(
        hidden_kernel,
        (shape(tokens, width, BF),) + sums,
        core_at,
        lengths,
        *hidden_near,
        *hidden_away,
        pulled,
        act_near,
        act_away,
        smem=2,
        flops=2 * tokens * width * units,
    )
    up_send, up_keep = call(
        weights_kernel,
        sums,
        core_at,
        grad_hidden,
        down_weight,
        slope_near,
        slope_away,
        normed_near,
        normed_away,
        scratch=[pltpu.VMEM((tokens, units), BF)],
        smem=1,
        flops=4 * tokens * width * units,
    )
    down_terms = sum_img_start(down_send, down_keep, y_at)
    up_terms = sum_img_start(up_send, up_keep, y_at)
    down_grad = sum_img_end(down_terms, z_at).T
    up_grad = sum_img_end(up_terms, z_at)

    grad_high, grad_low = after(grad_high, up_terms[1]), after(grad_low, up_terms[1])
    grad_image_unit = logit_scale * (
        lax.dot_general(grad_high, text_send, OVER_ROWS, preferred_element_type=F32)
        + lax.dot_general(grad_low, text_send, OVER_ROWS, preferred_element_type=F32)
    )
    grad_image_raw = unit_back(grad_image_unit, image_unit, image_inv).astype(BF)
    columns = grad_image_raw.shape[1] // 32
    chosen = jnp.arange(grad_image_raw.shape[1])[:, None] == (
        img * columns + jnp.arange(columns)[None, :]
    )
    own_columns = jnp.dot(
        grad_image_raw, chosen.astype(BF), preferred_element_type=F32
    ).astype(BF)
    projected = lax.dot_general(image_normed, own_columns, OVER_ROWS, preferred_element_type=F32)
    rows = image_width // 8
    image_proj_grad = lax.dynamic_slice_in_dim(projected, txt * rows, rows, axis=0)
    return (image_proj_grad, up_grad, down_grad)


def solution(mesh):
    return jax.shard_map(
        body,
        mesh=mesh,
        in_specs=(
            P(("img", "txt"), None, None),
            P(("img", "txt")),
            P(("img", "txt")),
            P(),
            P(None, "txt"),
            P("txt", None),
            P(),
            P(),
            P(("img", "txt"), None),
            P(),
            P(),
            P(),
        ),
        out_specs=(P("txt", "img"), P("img", "txt"), P("txt", "img")),
        check_vma=False,
    )
```

```python
import jax
import jax.numpy as jnp
from jax import lax
from jax.experimental import pallas as pl
from jax.experimental.pallas import tpu as pltpu
from jax.sharding import PartitionSpec as P

EPSILON = 1e-05
ROOT_HALF = 0.7071067811865476
INV_ROOT_TAU = 0.3989422804014327
BF = jnp.bfloat16
F32 = jnp.float32
PAD = 80


def centre(values):
    return values - jnp.mean(values, axis=-1, keepdims=True)


def inv_std_of(centred):
    return lax.rsqrt(jnp.mean(centred * centred, axis=-1, keepdims=True) + EPSILON)


def unit_rows(raw):
    inv_norm = lax.rsqrt(jnp.sum(raw * raw, axis=-1, keepdims=True) + 1e-06)
    return (raw * inv_norm, inv_norm)


def unit_back(grad_unit, direction, inv_norm):
    return inv_norm * (
        grad_unit - direction * jnp.sum(direction * grad_unit, axis=-1, keepdims=True)
    )


VMEM_LIMIT = 40 * 1024 * 1024
OVER_ROWS = (((0,), (0,)), ((), ()))
OVER_COLS = (((1,), (1,)), ((), ()))


def call(kernel, outs, *operands, scratch=(), smem=0, flops=0):
    size = sum(v.size * v.dtype.itemsize for v in operands) + sum(
        v.size * v.dtype.itemsize for v in outs
    )
    specs = [pl.BlockSpec(memory_space=pltpu.SMEM)] * smem
    specs += [pl.BlockSpec(memory_space=pltpu.VMEM)] * (len(operands) - smem)
    return pl.pallas_call(
        kernel,
        out_shape=outs,
        in_specs=specs,
        out_specs=[pl.BlockSpec(memory_space=pltpu.VMEM)] * len(outs),
        scratch_shapes=list(scratch),
        cost_estimate=pl.CostEstimate(flops=flops, bytes_accessed=size, transcendentals=0),
        compiler_params=pltpu.CompilerParams(vmem_limit_bytes=VMEM_LIMIT),
    )(*operands)


def shape(rows, cols, dtype):
    return jax.ShapeDtypeStruct((rows, cols), dtype)


def padded(states_ref, slot, scratch):
    length = states_ref.shape[1]
    scratch[PAD - 8 :, :] = jnp.zeros((8, scratch.shape[1]), F32)
    scratch[:length, :] = states_ref[slot].astype(F32)
    return scratch[...]


def norm_kernel(count_ref, length_ref, states_ref, image_ref, gain_ref, out_ref, scratch):
    length = states_ref.shape[1]
    width = out_ref.shape[1]
    rest = image_ref.shape[1] - width
    lane = lax.broadcasted_iota(jnp.int32, (1, 128), 1)
    image = image_ref[...].astype(F32)
    for slot in range(states_ref.shape[0]):
        centred = centre(padded(states_ref, slot, scratch))
        scratch[...] = centred * inv_std_of(centred) * gain_ref[...]
        valid = (slot < count_ref[0]).astype(F32)
        flags = jnp.where(lane == 0, valid, length_ref[slot].astype(F32))
        scratch[length : length + 1, :] = image[slot : slot + 1, :width]
        scratch[length + 1 : length + 2, :rest] = image[slot : slot + 1, width:]
        scratch[length + 1 : length + 2, rest : rest + 128] = jnp.where(lane < 2, flags, 0.0)
        out_ref[slot * PAD : (slot + 1) * PAD, :] = scratch[...].astype(BF)


def forward_kernel(
    own_ref, left_ref, right_ref, far_ref, up_ref, down_ref,
    normed_ref, act_ref, slope_ref, image_ref, o_own, o_left, o_right, o_far_a, o_far_b,
):
    rows = own_ref.shape[0]
    image = []
    for k, ref in enumerate((own_ref, left_ref, right_ref, far_ref)):
        normed_ref[k * rows : (k + 1) * rows, :] = ref[...]
        for end in range(PAD, rows + 1, PAD):
            last = ref[end - 16 : end, :].astype(F32)
            image.append(jnp.concatenate([last[13:14, :], last[14:15, :512]], axis=1))
    image_ref[...] = jnp.concatenate(image, axis=0).astype(BF)
    for part in range(2):
        span = slice(2 * part * rows, 2 * (part + 1) * rows)
        preact = jnp.dot(normed_ref[span, :], up_ref[...], preferred_element_type=F32)
        cdf = 0.5 * (1.0 + lax.erf(preact * ROOT_HALF))
        act_ref[span, :] = (preact * cdf).astype(BF)
        slope = cdf + preact * INV_ROOT_TAU * jnp.exp(-0.5 * preact * preact)
        slope_ref[span, :] = slope.astype(BF)
        out = jnp.dot(act_ref[span, :], down_ref[...], preferred_element_type=F32)
        if part == 0:
            o_own[...] = out[:rows]
            o_left[...] = out[rows:]
        else:
            o_right[...] = out[:rows]
            o_far_a[...] = out[rows : rows + rows // 2].astype(BF)
            o_far_b[...] = out[rows + rows // 2 :].astype(BF)


def relay_kernel(left_ref, right_ref, got_a_ref, got_b_ref, o_left, o_right):
    half = got_a_ref.shape[0]
    o_right[:half, :] = (right_ref[:half, :] + got_a_ref[...].astype(F32)).astype(BF)
    o_right[half:, :] = right_ref[half:, :].astype(BF)
    o_left[:half, :] = left_ref[:half, :].astype(BF)
    o_left[half:, :] = (left_ref[half:, :] + got_b_ref[...].astype(F32)).astype(BF)


def away_kernel(own_ref, left_ref, right_ref, out_ref):
    total = own_ref[...] + left_ref[...].astype(F32) + right_ref[...].astype(F32)
    out_ref[...] = total.astype(BF)


def final_kernel(
    length_ref, states_ref, own_ref, left_ref, right_ref, away_ref, gain_ref,
    pooled_ref, centred_ref, scratch,
):
    pooled = []
    for slot in range(states_ref.shape[0]):
        span = slice(slot * PAD, (slot + 1) * PAD)
        total = own_ref[span, :] + left_ref[span, :].astype(F32) + right_ref[span, :].astype(F32)
        total = total + away_ref[span, :].astype(F32)
        centred = centre(padded(states_ref, slot, scratch) + total)
        centred_ref[span, :] = centred.astype(BF)
        count = length_ref[slot]
        kept = (lax.broadcasted_iota(jnp.int32, (PAD, 1), 0) < count).astype(F32)
        weight = kept * inv_std_of(centred) / count.astype(F32)
        pooled.append(jnp.sum(centred * weight, axis=0, keepdims=True) * gain_ref[...])
    pooled_ref[...] = jnp.concatenate(pooled, axis=0).astype(BF)


def split_core(core, rows, part, send_ref, keep_ref):
    run = 40
    for j in range(rows.shape[0] // (4 * run)):
        first = rows[j * 4 * run : j * 4 * run + run]
        second = rows[j * 4 * run + run : j * 4 * run + 2 * run]
        third = rows[j * 4 * run + 2 * run : j * 4 * run + 3 * run]
        fourth = rows[j * 4 * run + 3 * run : j * 4 * run + 4 * run]
        even = jnp.concatenate([first, third], axis=0)
        odd = jnp.concatenate([second, fourth], axis=0)
        base = part * rows.shape[0] // 2 + j * 2 * run
        span = slice(base, base + 2 * run)
        send_ref[span, :] = jnp.where(core == 0, odd, even).astype(BF)
        keep_ref[span, :] = jnp.where(core == 0, even, odd)


def hidden_kernel(
    core_ref, length_ref, h0, h1, h2, h3, h4, h5, h6, h7, pulled_ref, act_a_ref, act_b_ref,
    grad_ref, send_ref, keep_ref,
):
    place = 0
    for ref in (h0, h1, h2, h3, h4, h5, h6, h7):
        grad_ref[place : place + ref.shape[0], :] = ref[...]
        place += ref.shape[0]

    def sample(index, carry):
        span = pl.ds(pl.multiple_of(index * PAD, PAD), PAD)
        centred = grad_ref[span, :].astype(F32)
        inv = inv_std_of(centred)
        hat = centred * inv
        pulled = pulled_ref[pl.ds(index, 1), :]
        along = jnp.mean(pulled * hat, axis=-1, keepdims=True)
        count = length_ref[index]
        kept = (lax.broadcasted_iota(jnp.int32, (PAD, 1), 0) < count).astype(F32)
        weight = kept * inv / count.astype(F32)
        grad = weight * (pulled - jnp.mean(pulled, axis=-1, keepdims=True) - hat * along)
        grad_ref[span, :] = grad.astype(BF)
        return carry

    lax.fori_loop(0, place // PAD, sample, 0)
    tokens = act_a_ref.shape[0]
    for part in range(2):
        cols = slice(part * 640, (part + 1) * 640)
        rows = lax.dot_general(
            grad_ref[:tokens, cols], act_a_ref[...], OVER_ROWS, preferred_element_type=F32
        ) + lax.dot_general(
            grad_ref[tokens:, cols], act_b_ref[...], OVER_ROWS, preferred_element_type=F32
        )
        split_core(core_ref[0], rows, part, send_ref, keep_ref)


def weights_kernel(
    core_ref, grad_ref, down_ref, slope_a_ref, slope_b_ref, normed_a_ref, normed_b_ref,
    send_ref, keep_ref, scratch,
):
    tokens = slope_a_ref.shape[0]
    for part, slope_ref in enumerate((slope_a_ref, slope_b_ref)):
        span = slice(part * tokens, (part + 1) * tokens)
        back = lax.dot_general(
            grad_ref[span, :], down_ref[...], OVER_COLS, preferred_element_type=F32
        )
        scratch[span, :] = (back * slope_ref[...].astype(F32)).astype(BF)
    for part in range(2):
        cols = slice(part * 640, (part + 1) * 640)
        rows = lax.dot_general(
            normed_a_ref[:, cols], scratch[:tokens, :], OVER_ROWS, preferred_element_type=F32
        ) + lax.dot_general(
            normed_b_ref[:, cols], scratch[tokens:, :], OVER_ROWS, preferred_element_type=F32
        )
        split_core(core_ref[0], rows, part, send_ref, keep_ref)


def spread_y_kernel(y_ref, keep_ref, got_ref, own_ref, s1_ref, s2_ref, s3_ref, scratch):
    scratch[...] = keep_ref[...] + got_ref[...].astype(F32)
    for shift, ref in ((0, own_ref), (1, s1_ref), (3, s2_ref), (2, s3_ref)):
        place = lax.rem(y_ref[0] + shift, 4) * 40
        for pair in range(2):
            runs = [
                scratch[pl.ds(pl.multiple_of((2 * pair + k) * 160 + place, 8), 40), :]
                for k in range(2)
            ]
            ref[pair * 80 : (pair + 1) * 80, :] = jnp.concatenate(runs, axis=0).astype(ref.dtype)


def spread_z_kernel(z_ref, keep_ref, r1_ref, r2_ref, r3_ref, own_ref, s1_ref, s2_ref, s3_ref, scratch):
    scratch[...] = (
        keep_ref[...]
        + r1_ref[...].astype(F32)
        + r2_ref[...].astype(F32)
        + r3_ref[...].astype(F32)
    )
    for shift, ref in ((0, own_ref), (1, s1_ref), (3, s2_ref), (2, s3_ref)):
        place = lax.rem(z_ref[0] + shift, 4) * 40
        ref[...] = scratch[pl.ds(pl.multiple_of(place, 8), 40), :].astype(ref.dtype)


def move_txt(value, z_hi=0, x=0):
    pairs = [
        (a * 4 + b, ((a + z_hi) % 2) * 4 + (b + x) % 4) for a in range(2) for b in range(4)
    ]
    return lax.ppermute(value, "txt", pairs)


def move_img(value, z_lo=0, y=0, core=0):
    pairs = [
        (a * 8 + b * 2 + c, ((a + z_lo) % 4) * 8 + ((b + y) % 4) * 2 + (c + core) % 2)
        for a in range(4)
        for b in range(4)
        for c in range(2)
    ]
    return lax.ppermute(value, "img", pairs)


def after(value, *events):
    return lax.optimization_barrier((value,) + events)[0]


def nought(*events):
    return sum(event[0, 0].astype(F32) for event in events) * 0.0


def joined(*rows):
    return lax.optimization_barrier(jnp.concatenate(rows, axis=0))


def gather_txt(rows):
    rows = joined(rows, move_txt(rows, x=1), move_txt(rows, x=-1), move_txt(rows, x=2))
    return joined(rows, move_txt(rows, z_hi=1))


def gather_z(rows):
    return joined(rows, move_img(rows, z_lo=1), move_img(rows, z_lo=-1), move_img(rows, z_lo=2))


def gather_y(rows):
    return joined(rows, move_img(rows, y=1), move_img(rows, y=-1), move_img(rows, y=2))


def gather_core(rows):
    return jnp.concatenate([rows, move_img(rows, core=1)], axis=0)


def ring_x(piece, way):
    left, right = move_txt(piece, x=1), move_txt(piece, x=-1)
    return piece, left, right, move_txt(left if way > 0 else right, x=way)


def ring_x_back(terms):
    own, left, right, far_a, far_b = terms
    got_a = move_txt(far_a, x=1)
    got_b = move_txt(far_b, x=-1)
    left, right = call(
        relay_kernel, (shape(left.shape[0], left.shape[1], BF),) * 2, left, right, got_a, got_b
    )
    return own, move_txt(right, x=1), move_txt(left, x=-1)


def forward(pieces, up_weight, down_weight):
    rows = pieces[0].shape[0]
    tokens = 4 * rows
    width, units = up_weight.shape
    return call(
        forward_kernel,
        (
            shape(tokens, width, BF),
            shape(tokens, units, BF),
            shape(tokens, units, BF),
            shape(tokens // PAD, width + 512, BF),
        )
        + (shape(rows, width, F32),) * 3
        + (shape(rows // 2, width, BF),) * 2,
        *pieces,
        up_weight,
        down_weight,
        flops=4 * tokens * width * units,
    )


def sum_img_start(send, keep, y):
    got = move_img(send, core=1)
    cols = keep.shape[1]
    outs = (shape(160, cols, F32),) + (shape(160, cols, BF),) * 3
    own, s1, s2, s3 = call(
        spread_y_kernel, outs, y, keep, got, scratch=[pltpu.VMEM(keep.shape, F32)], smem=1
    )
    return own, s1, s2, s3


def sum_img_end(terms, z_lo):
    own, s1, s2, s3 = terms
    cols = own.shape[1]
    s3, s1, s2 = move_img(s3, y=2), move_img(s1, y=1), move_img(s2, y=-1)
    outs = (shape(40, cols, F32),) + (shape(40, cols, BF),) * 3
    own, s1, s2, s3 = call(
        spread_z_kernel, outs, z_lo, own, s1, s2, s3,
        scratch=[pltpu.VMEM((160, cols), F32)], smem=1,
    )
    s3, s1, s2 = move_img(s3, z_lo=2), move_img(s1, z_lo=1), move_img(s2, z_lo=-1)
    return own + s1.astype(F32) + s2.astype(F32) + s3.astype(F32)


def body(
    text_states,
    text_length,
    sample_count,
    mlp_gain,
    up_weight,
    down_weight,
    final_gain,
    text_proj,
    image_pooled,
    image_gain,
    image_proj,
    logit_scale,
):
    samples, length, width = text_states.shape
    image_width = image_pooled.shape[1]
    txt = lax.axis_index("txt")
    img = lax.axis_index("img")
    z_lo, y, core = img // 8, (img // 2) % 4, img % 2

    row_gain = mlp_gain.reshape(1, width)
    row_final = final_gain.reshape(1, width)

    rows = samples * PAD
    padding = pltpu.VMEM((PAD, width), F32)
    (normed_own,) = call(
        norm_kernel,
        (shape(rows, width, BF),),
        sample_count,
        text_length,
        text_states,
        image_pooled,
        row_gain,
        scratch=[padding],
        smem=2,
    )
    near = ring_x(normed_own, 1)
    normed_far = after(move_txt(normed_own, z_hi=1), near[1])
    away = ring_x(normed_far, -1)
    normed_near, act_near, slope_near, image_near, *terms_near = forward(
        near, up_weight, down_weight
    )
    normed_away, act_away, slope_away, image_away, *terms_away = forward(
        away, up_weight, down_weight
    )
    image_rows = gather_z(joined(image_near, image_away))
    terms_away = ring_x_back(terms_away)
    terms_near = ring_x_back(terms_near)
    (away_sum,) = call(away_kernel, (shape(rows, width, BF),), *terms_away)
    from_away = move_txt(away_sum, z_hi=1)
    image_rows = gather_y(image_rows)
    image_all = gather_core(image_rows)

    pooled, hidden = call(
        final_kernel,
        (shape(samples, width, BF), shape(rows, width, BF)),
        text_length,
        text_states,
        *terms_near,
        from_away,
        row_final,
        scratch=[padding],
        smem=1,
    )
    pooled_z = gather_z(gather_txt(pooled))
    hidden_near = ring_x(hidden, 1)
    hidden_away = ring_x(move_txt(hidden, z_hi=1), -1)
    pooled_y = gather_y(pooled_z + nought(hidden_near[1], hidden_near[2]).astype(BF))

    valid = image_all[:, image_width] > 0.5
    lengths = image_all[: 8 * samples, image_width + 1].astype(jnp.int32)
    image_centred = centre(image_all[:, :image_width].astype(F32))
    image_normed = (image_centred * inv_std_of(image_centred) * image_gain).astype(BF)
    image_raw = jnp.dot(image_normed, image_proj, preferred_element_type=F32)
    image_unit, image_inv = unit_rows(image_raw)
    image_send = image_unit.astype(BF)

    pooled_all = gather_core(pooled_y + nought(hidden_away[1], hidden_away[2]).astype(BF))
    scale = logit_scale + nought(image_send)

    group = 8 * samples
    text_raw = jnp.dot(pooled_all, text_proj, preferred_element_type=F32)
    text_unit, text_inv = unit_rows(text_raw)
    text_send = text_unit.astype(BF)
    scores = scale * lax.dot_general(
        text_send, image_send, OVER_COLS, preferred_element_type=F32
    )
    batch = scores.shape[0]

    def masked_logsum(axis, mask):
        top = jnp.max(jnp.where(mask, scores, -1e30), axis=axis, keepdims=True)
        total = jnp.sum(jnp.exp(jnp.where(mask, scores - top, -1e30)), axis=axis, keepdims=True)
        return top + jnp.log(total)

    row_lse = masked_logsum(0, valid[:, None])
    col_lse = masked_logsum(1, valid[None, :])
    pair_mask = valid[:, None] & valid[None, :]
    row_prob = jnp.exp(jnp.where(pair_mask, scores - row_lse, -1e30))
    col_prob = jnp.exp(jnp.where(pair_mask, scores - col_lse, -1e30))
    same = jnp.arange(batch)[:, None] == jnp.arange(batch)[None, :]
    grad_scores = 0.5 * (row_prob + col_prob) - jnp.where(pair_mask & same, 1.0, 0.0)
    grad_high = lax.reduce_precision(grad_scores, 8, 7)
    grad_low = (grad_scores - grad_high).astype(BF)
    grad_high = grad_high.astype(BF)

    grad_text_unit = (logit_scale + nought(hidden_near[3], hidden_away[3])) * (
        jnp.dot(grad_high[:group], image_send, preferred_element_type=F32)
        + jnp.dot(grad_low[:group], image_send, preferred_element_type=F32)
    )
    grad_text_raw = unit_back(grad_text_unit, text_unit[:group], text_inv[:group]).astype(BF)
    grad_pooled = lax.dot_general(
        grad_text_raw, text_proj, OVER_COLS, preferred_element_type=F32
    )
    pulled = grad_pooled * final_gain
    core_at, y_at, z_at = (v.reshape(1).astype(jnp.int32) for v in (core, y, z_lo))
    units = act_near.shape[1]
    tokens = group * PAD
    sums = (shape(width // 2, units, BF), shape(width // 2, units, F32))
    grad_hidden, down_send, down_keep = call(
        hidden_kernel,
        (shape(tokens, width, BF),) + sums,
        core_at,
        lengths,
        *hidden_near,
        *hidden_away,
        pulled,
        act_near,
        act_away,
        smem=2,
        flops=2 * tokens * width * units,
    )
    up_send, up_keep = call(
        weights_kernel,
        sums,
        core_at,
        grad_hidden,
        down_weight,
        slope_near,
        slope_away,
        normed_near,
        normed_away,
        scratch=[pltpu.VMEM((tokens, units), BF)],
        smem=1,
        flops=4 * tokens * width * units,
    )
    down_terms = sum_img_start(down_send, down_keep, y_at)
    up_terms = sum_img_start(up_send, up_keep, y_at)
    down_grad = sum_img_end(down_terms, z_at).T
    up_grad = sum_img_end(up_terms, z_at)

    grad_high, grad_low = after(grad_high, up_terms[1]), after(grad_low, up_terms[1])
    grad_image_unit = logit_scale * (
        lax.dot_general(grad_high, text_send, OVER_ROWS, preferred_element_type=F32)
        + lax.dot_general(grad_low, text_send, OVER_ROWS, preferred_element_type=F32)
    )
    grad_image_raw = unit_back(grad_image_unit, image_unit, image_inv).astype(BF)
    columns = grad_image_raw.shape[1] // 32
    chosen = jnp.arange(grad_image_raw.shape[1])[:, None] == (
        img * columns + jnp.arange(columns)[None, :]
    )
    own_columns = jnp.dot(
        grad_image_raw, chosen.astype(BF), preferred_element_type=F32
    ).astype(BF)
    projected = lax.dot_general(image_normed, own_columns, OVER_ROWS, preferred_element_type=F32)
    rows = image_width // 8
    image_proj_grad = lax.dynamic_slice_in_dim(projected, txt * rows, rows, axis=0)
    return (image_proj_grad, up_grad, down_grad)


def solution(mesh):
    return jax.shard_map(
        body,
        mesh=mesh,
        in_specs=(
            P(("img", "txt"), None, None),
            P(("img", "txt")),
            P(("img", "txt")),
            P(),
            P(None, "txt"),
            P("txt", None),
            P(),
            P(),
            P(("img", "txt"), None),
            P(),
            P(),
            P(),
        ),
        out_specs=(P("txt", "img"), P("img", "txt"), P("txt", "img")),
        check_vma=False,
    )
```

```python
import jax
import jax.numpy as jnp
from jax import lax
from jax.experimental import pallas as pl
from jax.experimental.pallas import tpu as pltpu
from jax.sharding import PartitionSpec as P

EPSILON = 1e-05
ROOT_HALF = 0.7071067811865476
INV_ROOT_TAU = 0.3989422804014327
BF = jnp.bfloat16
F32 = jnp.float32
PAD = 80


def centre(values):
    return values - jnp.mean(values, axis=-1, keepdims=True)


def inv_std_of(centred):
    return lax.rsqrt(jnp.mean(centred * centred, axis=-1, keepdims=True) + EPSILON)


def unit_rows(raw):
    inv_norm = lax.rsqrt(jnp.sum(raw * raw, axis=-1, keepdims=True) + 1e-06)
    return (raw * inv_norm, inv_norm)


def unit_back(grad_unit, direction, inv_norm):
    return inv_norm * (
        grad_unit - direction * jnp.sum(direction * grad_unit, axis=-1, keepdims=True)
    )


VMEM_LIMIT = 40 * 1024 * 1024
OVER_ROWS = (((0,), (0,)), ((), ()))
OVER_COLS = (((1,), (1,)), ((), ()))


def call(kernel, outs, *operands, scratch=(), smem=0, anywhere=0, flops=0):
    size = sum(v.size * v.dtype.itemsize for v in operands) + sum(
        v.size * v.dtype.itemsize for v in outs
    )
    specs = [pl.BlockSpec(memory_space=pltpu.SMEM)] * smem
    specs += [pl.BlockSpec(memory_space=pl.ANY)] * anywhere
    specs += [pl.BlockSpec(memory_space=pltpu.VMEM)] * (len(operands) - smem - anywhere)
    return pl.pallas_call(
        kernel,
        out_shape=outs,
        in_specs=specs,
        out_specs=[pl.BlockSpec(memory_space=pltpu.VMEM)] * len(outs),
        scratch_shapes=list(scratch),
        cost_estimate=pl.CostEstimate(flops=flops, bytes_accessed=size, transcendentals=0),
        compiler_params=pltpu.CompilerParams(vmem_limit_bytes=VMEM_LIMIT),
    )(*operands)


def shape(rows, cols, dtype):
    return jax.ShapeDtypeStruct((rows, cols), dtype)


def padded(states_ref, slot, scratch):
    length = states_ref.shape[1]
    scratch[PAD - 8 :, :] = jnp.zeros((8, scratch.shape[1]), F32)
    scratch[:length, :] = states_ref[slot].astype(F32)
    return scratch[...]


def norm_kernel(count_ref, length_ref, states_ref, image_ref, gain_ref, out_ref, scratch):
    length = states_ref.shape[1]
    width = out_ref.shape[1]
    rest = image_ref.shape[1] - width
    lane = lax.broadcasted_iota(jnp.int32, (1, 128), 1)
    image = image_ref[...].astype(F32)
    for slot in range(states_ref.shape[0]):
        centred = centre(padded(states_ref, slot, scratch))
        scratch[...] = centred * inv_std_of(centred) * gain_ref[...]
        valid = (slot < count_ref[0]).astype(F32)
        flags = jnp.where(lane == 0, valid, length_ref[slot].astype(F32))
        scratch[length : length + 1, :] = image[slot : slot + 1, :width]
        scratch[length + 1 : length + 2, :rest] = image[slot : slot + 1, width:]
        scratch[length + 1 : length + 2, rest : rest + 128] = jnp.where(lane < 2, flags, 0.0)
        out_ref[slot * PAD : (slot + 1) * PAD, :] = scratch[...].astype(BF)


def forward_kernel(
    own_ref, left_ref, right_ref, far_ref, up_ref, down_ref,
    normed_ref, act_ref, slope_ref, image_ref, o_own, o_left, o_right, o_far_a, o_far_b,
):
    rows = own_ref.shape[0]
    image = []
    for k, ref in enumerate((own_ref, left_ref, right_ref, far_ref)):
        normed_ref[k * rows : (k + 1) * rows, :] = ref[...]
        for end in range(PAD, rows + 1, PAD):
            last = ref[end - 16 : end, :].astype(F32)
            image.append(jnp.concatenate([last[13:14, :], last[14:15, :512]], axis=1))
    image_ref[...] = jnp.concatenate(image, axis=0).astype(BF)
    for part in range(2):
        span = slice(2 * part * rows, 2 * (part + 1) * rows)
        preact = jnp.dot(normed_ref[span, :], up_ref[...], preferred_element_type=F32)
        cdf = 0.5 * (1.0 + lax.erf(preact * ROOT_HALF))
        act_ref[span, :] = (preact * cdf).astype(BF)
        slope = cdf + preact * INV_ROOT_TAU * jnp.exp(-0.5 * preact * preact)
        slope_ref[span, :] = slope.astype(BF)
        out = jnp.dot(act_ref[span, :], down_ref[...], preferred_element_type=F32)
        if part == 0:
            o_own[...] = out[:rows]
            o_left[...] = out[rows:]
        else:
            o_right[...] = out[:rows]
            o_far_a[...] = out[rows : rows + rows // 2].astype(BF)
            o_far_b[...] = out[rows + rows // 2 :].astype(BF)


def relay_kernel(left_ref, right_ref, got_a_ref, got_b_ref, o_left, o_right):
    half = got_a_ref.shape[0]
    o_right[:half, :] = (right_ref[:half, :] + got_a_ref[...].astype(F32)).astype(BF)
    o_right[half:, :] = right_ref[half:, :].astype(BF)
    o_left[:half, :] = left_ref[:half, :].astype(BF)
    o_left[half:, :] = (left_ref[half:, :] + got_b_ref[...].astype(F32)).astype(BF)


def away_kernel(own_ref, left_ref, right_ref, out_ref):
    total = own_ref[...] + left_ref[...].astype(F32) + right_ref[...].astype(F32)
    out_ref[...] = total.astype(BF)


def final_kernel(
    length_ref, states_ref, own_ref, left_ref, right_ref, away_ref, gain_ref,
    pooled_ref, centred_ref, half_a_ref, half_b_ref, scratch,
):
    pooled = []
    for slot in range(states_ref.shape[0]):
        span = slice(slot * PAD, (slot + 1) * PAD)
        total = own_ref[span, :] + left_ref[span, :].astype(F32) + right_ref[span, :].astype(F32)
        total = total + away_ref[span, :].astype(F32)
        centred = centre(padded(states_ref, slot, scratch) + total)
        centred_ref[span, :] = centred.astype(BF)
        (half_a_ref, half_b_ref)[slot][...] = centred.astype(BF)
        count = length_ref[slot]
        kept = (lax.broadcasted_iota(jnp.int32, (PAD, 1), 0) < count).astype(F32)
        weight = kept * inv_std_of(centred) / count.astype(F32)
        pooled.append(jnp.sum(centred * weight, axis=0, keepdims=True) * gain_ref[...])
    pooled_ref[...] = jnp.concatenate(pooled, axis=0).astype(BF)


def split_core(core, rows, part, send_ref, keep_ref):
    run = 40
    for j in range(rows.shape[0] // (4 * run)):
        first = rows[j * 4 * run : j * 4 * run + run]
        second = rows[j * 4 * run + run : j * 4 * run + 2 * run]
        third = rows[j * 4 * run + 2 * run : j * 4 * run + 3 * run]
        fourth = rows[j * 4 * run + 3 * run : j * 4 * run + 4 * run]
        even = jnp.concatenate([first, third], axis=0)
        odd = jnp.concatenate([second, fourth], axis=0)
        base = part * rows.shape[0] // 2 + j * 2 * run
        span = slice(base, base + 2 * run)
        send_ref[span, :] = jnp.where(core == 0, odd, even).astype(BF)
        keep_ref[span, :] = jnp.where(core == 0, even, odd).astype(BF)


def hidden_kernel(
    core_ref, length_ref, h0, h1, h2, h3, h4, h5, h6, h7, pulled_ref, act_a_ref, act_b_ref,
    grad_ref, send_ref, keep_ref, hidden_ref, arrived,
):
    rows = h0.shape[0]
    pieces = [
        pltpu.make_async_copy(ref, hidden_ref.at[pl.ds(k * rows, rows)], arrived.at[k])
        for k, ref in enumerate((h0, h1, h2, h3, h4, h5, h6, h7))
    ]
    for piece in pieces:
        piece.start()
    for piece in pieces:
        piece.wait()

    def sample(index, carry):
        span = pl.ds(pl.multiple_of(index * PAD, PAD), PAD)
        centred = hidden_ref[span, :].astype(F32)
        inv = inv_std_of(centred)
        hat = centred * inv
        pulled = pulled_ref[pl.ds(index, 1), :]
        along = jnp.mean(pulled * hat, axis=-1, keepdims=True)
        count = length_ref[index]
        kept = (lax.broadcasted_iota(jnp.int32, (PAD, 1), 0) < count).astype(F32)
        weight = kept * inv / count.astype(F32)
        grad = weight * (pulled - jnp.mean(pulled, axis=-1, keepdims=True) - hat * along)
        grad_ref[span, :] = grad.astype(BF)
        return carry

    lax.fori_loop(0, grad_ref.shape[0] // PAD, sample, 0)
    tokens = act_a_ref.shape[0]
    for part in range(2):
        cols = slice(part * 640, (part + 1) * 640)
        rows = lax.dot_general(
            grad_ref[:tokens, cols], act_a_ref[...], OVER_ROWS, preferred_element_type=F32
        ) + lax.dot_general(
            grad_ref[tokens:, cols], act_b_ref[...], OVER_ROWS, preferred_element_type=F32
        )
        split_core(core_ref[0], rows, part, send_ref, keep_ref)


def weights_kernel(
    core_ref, grad_ref, down_ref, slope_a_ref, slope_b_ref, normed_a_ref, normed_b_ref,
    send_ref, keep_ref, scratch,
):
    tokens = slope_a_ref.shape[0]
    for part, slope_ref in enumerate((slope_a_ref, slope_b_ref)):
        span = slice(part * tokens, (part + 1) * tokens)
        back = lax.dot_general(
            grad_ref[span, :], down_ref[...], OVER_COLS, preferred_element_type=F32
        )
        scratch[span, :] = (back * slope_ref[...].astype(F32)).astype(BF)
    for part in range(2):
        cols = slice(part * 640, (part + 1) * 640)
        rows = lax.dot_general(
            normed_a_ref[:, cols], scratch[:tokens, :], OVER_ROWS, preferred_element_type=F32
        ) + lax.dot_general(
            normed_b_ref[:, cols], scratch[tokens:, :], OVER_ROWS, preferred_element_type=F32
        )
        split_core(core_ref[0], rows, part, send_ref, keep_ref)


def spread_y_kernel(y_ref, keep_ref, got_ref, own_ref, s1_ref, s2_ref, s3_ref, scratch):
    scratch[...] = keep_ref[...].astype(F32) + got_ref[...].astype(F32)
    for shift, ref in ((0, own_ref), (1, s1_ref), (3, s2_ref), (2, s3_ref)):
        place = lax.rem(y_ref[0] + shift, 4) * 40
        for pair in range(2):
            runs = [
                scratch[pl.ds(pl.multiple_of((2 * pair + k) * 160 + place, 8), 40), :]
                for k in range(2)
            ]
            ref[pair * 80 : (pair + 1) * 80, :] = jnp.concatenate(runs, axis=0).astype(ref.dtype)


def spread_z_kernel(z_ref, keep_ref, r1_ref, r2_ref, r3_ref, own_ref, s1_ref, s2_ref, s3_ref, scratch):
    scratch[...] = (
        keep_ref[...]
        + r1_ref[...].astype(F32)
        + r2_ref[...].astype(F32)
        + r3_ref[...].astype(F32)
    )
    for shift, ref in ((0, own_ref), (1, s1_ref), (3, s2_ref), (2, s3_ref)):
        place = lax.rem(z_ref[0] + shift, 4) * 40
        ref[...] = scratch[pl.ds(pl.multiple_of(place, 8), 40), :].astype(ref.dtype)


def move_txt(value, z_hi=0, x=0):
    pairs = [
        (a * 4 + b, ((a + z_hi) % 2) * 4 + (b + x) % 4) for a in range(2) for b in range(4)
    ]
    return lax.ppermute(value, "txt", pairs)


def move_img(value, z_lo=0, y=0, core=0):
    pairs = [
        (a * 8 + b * 2 + c, ((a + z_lo) % 4) * 8 + ((b + y) % 4) * 2 + (c + core) % 2)
        for a in range(4)
        for b in range(4)
        for c in range(2)
    ]
    return lax.ppermute(value, "img", pairs)


def nought(*events):
    return sum(event[0, 0].astype(F32) for event in events) * 0.0


def joined(*rows):
    return lax.optimization_barrier(jnp.concatenate(rows, axis=0))


def ring_txt(rows):
    return rows, move_txt(rows, x=1), move_txt(rows, x=-1), move_txt(rows, x=2)


def ring_z(rows):
    return rows, move_img(rows, z_lo=1), move_img(rows, z_lo=-1), move_img(rows, z_lo=2)


def ring_y(rows):
    return rows, move_img(rows, y=1), move_img(rows, y=-1), move_img(rows, y=2)


def gather_core(rows):
    return jnp.concatenate([rows, move_img(rows, core=1)], axis=0)


def ring_x(piece, way):
    left, right = move_txt(piece, x=1), move_txt(piece, x=-1)
    return piece, left, right, move_txt(left if way > 0 else right, x=way)


def ring_x_back(terms, held=None):
    own, left, right, far_a, far_b = terms
    got_a = move_txt(far_a, x=1)
    got_b = move_txt(far_b, x=-1)
    if held is not None:
        got_a, got_b, held = lax.optimization_barrier((got_a, got_b, held))
    left, right = call(
        relay_kernel, (shape(left.shape[0], left.shape[1], BF),) * 2, left, right, got_a, got_b
    )
    return (own, move_txt(right, x=1), move_txt(left, x=-1)), held


def forward(pieces, up_weight, down_weight):
    rows = pieces[0].shape[0]
    tokens = 4 * rows
    width, units = up_weight.shape
    return call(
        forward_kernel,
        (
            shape(tokens, width, BF),
            shape(tokens, units, BF),
            shape(tokens, units, BF),
            shape(tokens // PAD, width + 512, BF),
        )
        + (shape(rows, width, F32),) * 3
        + (shape(rows // 2, width, BF),) * 2,
        *pieces,
        up_weight,
        down_weight,
        flops=4 * tokens * width * units,
    )


def sum_img_start(send, keep, y):
    got = move_img(send, core=1)
    cols = keep.shape[1]
    outs = (shape(160, cols, F32),) + (shape(160, cols, BF),) * 3
    own, s1, s2, s3 = call(
        spread_y_kernel, outs, y, keep, got, scratch=[pltpu.VMEM(keep.shape, F32)], smem=1
    )
    return own, s1, s2, s3


def sum_img_end(terms, z_lo):
    own, s1, s2, s3 = terms
    cols = own.shape[1]
    s3, s1, s2 = move_img(s3, y=2), move_img(s1, y=1), move_img(s2, y=-1)
    outs = (shape(40, cols, F32),) + (shape(40, cols, BF),) * 3
    own, s1, s2, s3 = call(
        spread_z_kernel, outs, z_lo, own, s1, s2, s3,
        scratch=[pltpu.VMEM((160, cols), F32)], smem=1,
    )
    s3, s1, s2 = move_img(s3, z_lo=2), move_img(s1, z_lo=1), move_img(s2, z_lo=-1)
    return own + s1.astype(F32) + s2.astype(F32) + s3.astype(F32)


def body(
    text_states,
    text_length,
    sample_count,
    mlp_gain,
    up_weight,
    down_weight,
    final_gain,
    text_proj,
    image_pooled,
    image_gain,
    image_proj,
    logit_scale,
):
    samples, length, width = text_states.shape
    image_width = image_pooled.shape[1]
    txt = lax.axis_index("txt")
    img = lax.axis_index("img")
    z_lo, y, core = img // 8, (img // 2) % 4, img % 2

    row_gain = mlp_gain.reshape(1, width)
    row_final = final_gain.reshape(1, width)

    rows = samples * PAD
    padding = pltpu.VMEM((PAD, width), F32)
    (normed_own,) = call(
        norm_kernel,
        (shape(rows, width, BF),),
        sample_count,
        text_length,
        text_states,
        image_pooled,
        row_gain,
        scratch=[padding],
        smem=2,
    )
    near = ring_x(normed_own, 1)
    normed_far = move_txt(normed_own, z_hi=1) + nought(near[2]).astype(BF)
    away = ring_x(normed_far, -1)
    normed_near, act_near, slope_near, image_near, *terms_near = forward(
        near, up_weight, down_weight
    )
    normed_away, act_away, slope_away, image_away, *terms_away = forward(
        away, up_weight, down_weight
    )
    image_rows = jnp.concatenate([image_near, image_away], axis=0)
    image_rows = jnp.concatenate(ring_z(image_rows), axis=0)
    terms_away, image_rows = ring_x_back(terms_away, image_rows)
    terms_near, _ = ring_x_back(terms_near)
    (away_sum,) = call(away_kernel, (shape(rows, width, BF),), *terms_away)
    from_away, image_rows = lax.optimization_barrier(
        (move_txt(away_sum, z_hi=1), jnp.concatenate(ring_y(image_rows), axis=0))
    )

    pooled, hidden, half_a, half_b = call(
        final_kernel,
        (shape(samples, width, BF), shape(rows, width, BF)) + (shape(PAD, width, BF),) * 2,
        text_length,
        text_states,
        *terms_near,
        from_away,
        row_final,
        scratch=[padding],
        smem=1,
    )
    def together(*values):
        return lax.optimization_barrier(values)

    def rows_of(pieces):
        return jnp.concatenate(pieces, axis=0)

    pooled, hidden, half_a, half_b, image_rows = together(
        pooled, hidden, half_a, half_b, image_rows
    )
    left, right = move_txt(hidden, x=1), move_txt(hidden, x=-1)
    pooled_x, left, right, half_a, half_b, image_all = together(
        rows_of(ring_txt(pooled)), left, right, move_txt(half_a, z_hi=1), half_b,
        gather_core(image_rows),
    )
    pooled_txt, far, hidden_far, left, right = together(
        rows_of((pooled_x, move_txt(pooled_x, z_hi=1))), move_txt(left, x=1),
        rows_of((half_a, move_txt(half_b, z_hi=1))), left, right,
    )
    hidden_near = (hidden, left, right, far)
    pooled_z, far_left, far_right, hidden_far = together(
        rows_of(ring_z(pooled_txt)),
        move_txt(hidden_far, x=1), move_txt(hidden_far, x=-1), hidden_far,
    )
    pooled_y, far_far, far_left, far_right, hidden_far = together(
        rows_of(ring_y(pooled_z)), move_txt(far_right, x=-1), far_left, far_right, hidden_far
    )
    hidden_away = (hidden_far, far_left, far_right, far_far)

    valid = image_all[:, image_width] > 0.5
    lengths = image_all[: 8 * samples, image_width + 1].astype(jnp.int32)
    image_centred = centre(image_all[:, :image_width].astype(F32))
    image_normed = (image_centred * inv_std_of(image_centred) * image_gain).astype(BF)
    image_raw = jnp.dot(image_normed, image_proj, preferred_element_type=F32)
    image_unit, image_inv = unit_rows(image_raw)
    image_send = image_unit.astype(BF)

    pooled_all = gather_core(pooled_y)

    group = 8 * samples
    text_raw = jnp.dot(pooled_all, text_proj, preferred_element_type=F32)
    text_unit, text_inv = unit_rows(text_raw)
    text_send = text_unit.astype(BF)
    scores = logit_scale * lax.dot_general(
        text_send, image_send, OVER_COLS, preferred_element_type=F32
    )
    batch = scores.shape[0]

    def masked_logsum(axis, mask):
        top = jnp.max(jnp.where(mask, scores, -1e30), axis=axis, keepdims=True)
        total = jnp.sum(jnp.exp(jnp.where(mask, scores - top, -1e30)), axis=axis, keepdims=True)
        return top + jnp.log(total)

    row_lse = masked_logsum(0, valid[:, None])
    col_lse = masked_logsum(1, valid[None, :])
    pair_mask = valid[:, None] & valid[None, :]
    row_prob = jnp.exp(jnp.where(pair_mask, scores - row_lse, -1e30))
    col_prob = jnp.exp(jnp.where(pair_mask, scores - col_lse, -1e30))
    same = jnp.arange(batch)[:, None] == jnp.arange(batch)[None, :]
    grad_scores = 0.5 * (row_prob + col_prob) - jnp.where(pair_mask & same, 1.0, 0.0)
    grad_high = lax.reduce_precision(grad_scores, 8, 7)
    grad_low = (grad_scores - grad_high).astype(BF)
    grad_high = grad_high.astype(BF)

    grad_text_unit = logit_scale * (
        jnp.dot(grad_high[:group], image_send, preferred_element_type=F32)
        + jnp.dot(grad_low[:group], image_send, preferred_element_type=F32)
    )
    grad_text_raw = unit_back(grad_text_unit, text_unit[:group], text_inv[:group]).astype(BF)
    grad_pooled = lax.dot_general(
        grad_text_raw, text_proj, OVER_COLS, preferred_element_type=F32
    )
    pulled = grad_pooled * final_gain
    core_at, y_at, z_at = (v.reshape(1).astype(jnp.int32) for v in (core, y, z_lo))
    units = act_near.shape[1]
    tokens = group * PAD
    sums = (shape(width // 2, units, BF),) * 2
    grad_hidden, down_send, down_keep = call(
        hidden_kernel,
        (shape(tokens, width, BF),) + sums,
        core_at,
        lengths,
        *hidden_near,
        *hidden_away,
        pulled,
        act_near,
        act_away,
        scratch=[pltpu.VMEM((tokens, width), BF), pltpu.SemaphoreType.DMA((8,))],
        smem=2,
        anywhere=8,
        flops=2 * tokens * width * units,
    )
    up_send, up_keep = call(
        weights_kernel,
        sums,
        core_at,
        grad_hidden,
        down_weight,
        slope_near,
        slope_away,
        normed_near,
        normed_away,
        scratch=[pltpu.VMEM((tokens, units), BF)],
        smem=1,
        flops=4 * tokens * width * units,
    )
    down_terms = sum_img_start(down_send, down_keep, y_at)
    up_terms = sum_img_start(up_send, up_keep, y_at)
    down_grad = sum_img_end(down_terms, z_at).T
    up_grad = sum_img_end(up_terms, z_at)

    grad_image_unit = logit_scale * (
        lax.dot_general(grad_high, text_send, OVER_ROWS, preferred_element_type=F32)
        + lax.dot_general(grad_low, text_send, OVER_ROWS, preferred_element_type=F32)
    )
    grad_image_raw = unit_back(grad_image_unit, image_unit, image_inv).astype(BF)
    columns = grad_image_raw.shape[1] // 32
    chosen = jnp.arange(grad_image_raw.shape[1])[:, None] == (
        img * columns + jnp.arange(columns)[None, :]
    )
    own_columns = jnp.dot(
        grad_image_raw, chosen.astype(BF), preferred_element_type=F32
    ).astype(BF)
    projected = lax.dot_general(image_normed, own_columns, OVER_ROWS, preferred_element_type=F32)
    rows = image_width // 8
    image_proj_grad = lax.dynamic_slice_in_dim(projected, txt * rows, rows, axis=0)
    return (image_proj_grad, up_grad, down_grad)


def solution(mesh):
    return jax.shard_map(
        body,
        mesh=mesh,
        in_specs=(
            P(("img", "txt"), None, None),
            P(("img", "txt")),
            P(("img", "txt")),
            P(),
            P(None, "txt"),
            P("txt", None),
            P(),
            P(),
            P(("img", "txt"), None),
            P(),
            P(),
            P(),
        ),
        out_specs=(P("txt", "img"), P("img", "txt"), P("txt", "img")),
        check_vma=False,
    )
```

```python
import jax
import jax.numpy as jnp
from jax import lax
from jax.experimental import pallas as pl
from jax.experimental.pallas import tpu as pltpu
from jax.sharding import PartitionSpec as P

EPSILON = 1e-05
ROOT_HALF = 0.7071067811865476
INV_ROOT_TAU = 0.3989422804014327
BF = jnp.bfloat16
F32 = jnp.float32
PAD = 80


def centre(values):
    return values - jnp.mean(values, axis=-1, keepdims=True)


def inv_std_of(centred):
    return lax.rsqrt(jnp.mean(centred * centred, axis=-1, keepdims=True) + EPSILON)


def unit_rows(raw):
    inv_norm = lax.rsqrt(jnp.sum(raw * raw, axis=-1, keepdims=True) + 1e-06)
    return (raw * inv_norm, inv_norm)


def unit_back(grad_unit, direction, inv_norm):
    return inv_norm * (
        grad_unit - direction * jnp.sum(direction * grad_unit, axis=-1, keepdims=True)
    )


VMEM_LIMIT = 40 * 1024 * 1024
OVER_ROWS = (((0,), (0,)), ((), ()))
OVER_COLS = (((1,), (1,)), ((), ()))


def call(kernel, outs, *operands, scratch=(), smem=0, anywhere=0, flops=0):
    size = sum(v.size * v.dtype.itemsize for v in operands) + sum(
        v.size * v.dtype.itemsize for v in outs
    )
    specs = [pl.BlockSpec(memory_space=pltpu.SMEM)] * smem
    specs += [pl.BlockSpec(memory_space=pl.ANY)] * anywhere
    specs += [pl.BlockSpec(memory_space=pltpu.VMEM)] * (len(operands) - smem - anywhere)
    return pl.pallas_call(
        kernel,
        out_shape=outs,
        in_specs=specs,
        out_specs=[pl.BlockSpec(memory_space=pltpu.VMEM)] * len(outs),
        scratch_shapes=list(scratch),
        cost_estimate=pl.CostEstimate(flops=flops, bytes_accessed=size, transcendentals=0),
        compiler_params=pltpu.CompilerParams(vmem_limit_bytes=VMEM_LIMIT),
    )(*operands)


def shape(rows, cols, dtype):
    return jax.ShapeDtypeStruct((rows, cols), dtype)


def padded(states_ref, slot, scratch):
    length = states_ref.shape[1]
    scratch[PAD - 8 :, :] = jnp.zeros((8, scratch.shape[1]), F32)
    scratch[:length, :] = states_ref[slot].astype(F32)
    return scratch[...]


def norm_kernel(count_ref, length_ref, states_ref, image_ref, gain_ref, out_ref, scratch):
    length = states_ref.shape[1]
    width = out_ref.shape[1]
    rest = image_ref.shape[1] - width
    lane = lax.broadcasted_iota(jnp.int32, (1, 128), 1)
    image = image_ref[...].astype(F32)
    for slot in range(states_ref.shape[0]):
        centred = centre(padded(states_ref, slot, scratch))
        scratch[...] = centred * inv_std_of(centred) * gain_ref[...]
        valid = (slot < count_ref[0]).astype(F32)
        flags = jnp.where(lane == 0, valid, length_ref[slot].astype(F32))
        scratch[length : length + 1, :] = image[slot : slot + 1, :width]
        scratch[length + 1 : length + 2, :rest] = image[slot : slot + 1, width:]
        scratch[length + 1 : length + 2, rest : rest + 128] = jnp.where(lane < 2, flags, 0.0)
        out_ref[slot * PAD : (slot + 1) * PAD, :] = scratch[...].astype(BF)


def forward_kernel(
    own_ref, left_ref, right_ref, far_ref, up_ref, down_ref,
    normed_ref, act_ref, slope_ref, image_ref, o_own, o_left, o_right, o_far_a, o_far_b,
):
    rows = own_ref.shape[0]
    image = []
    for k, ref in enumerate((own_ref, left_ref, right_ref, far_ref)):
        normed_ref[k * rows : (k + 1) * rows, :] = ref[...]
        for end in range(PAD, rows + 1, PAD):
            last = ref[end - 16 : end, :].astype(F32)
            image.append(jnp.concatenate([last[13:14, :], last[14:15, :512]], axis=1))
    image_ref[...] = jnp.concatenate(image, axis=0).astype(BF)
    for part in range(2):
        span = slice(2 * part * rows, 2 * (part + 1) * rows)
        preact = jnp.dot(normed_ref[span, :], up_ref[...], preferred_element_type=F32)
        cdf = 0.5 * (1.0 + lax.erf(preact * ROOT_HALF))
        act_ref[span, :] = (preact * cdf).astype(BF)
        slope = cdf + preact * INV_ROOT_TAU * jnp.exp(-0.5 * preact * preact)
        slope_ref[span, :] = slope.astype(BF)
        out = jnp.dot(act_ref[span, :], down_ref[...], preferred_element_type=F32)
        if part == 0:
            o_own[...] = out[:rows]
            o_left[...] = out[rows:]
        else:
            o_right[...] = out[:rows]
            o_far_a[...] = out[rows : rows + rows // 2].astype(BF)
            o_far_b[...] = out[rows + rows // 2 :].astype(BF)


def relay_kernel(left_ref, right_ref, got_a_ref, got_b_ref, o_left, o_right):
    half = got_a_ref.shape[0]
    o_right[:half, :] = (right_ref[:half, :] + got_a_ref[...].astype(F32)).astype(BF)
    o_right[half:, :] = right_ref[half:, :].astype(BF)
    o_left[:half, :] = left_ref[:half, :].astype(BF)
    o_left[half:, :] = (left_ref[half:, :] + got_b_ref[...].astype(F32)).astype(BF)


def away_kernel(own_ref, left_ref, right_ref, out_ref):
    total = own_ref[...] + left_ref[...].astype(F32) + right_ref[...].astype(F32)
    out_ref[...] = total.astype(BF)


def final_kernel(
    length_ref, states_ref, own_ref, left_ref, right_ref, away_ref, gain_ref,
    pooled_ref, centred_ref, half_a_ref, half_b_ref, scratch,
):
    pooled = []
    for slot in range(states_ref.shape[0]):
        span = slice(slot * PAD, (slot + 1) * PAD)
        total = own_ref[span, :] + left_ref[span, :].astype(F32) + right_ref[span, :].astype(F32)
        total = total + away_ref[span, :].astype(F32)
        centred = centre(padded(states_ref, slot, scratch) + total)
        centred_ref[span, :] = centred.astype(BF)
        (half_a_ref, half_b_ref)[slot][...] = centred.astype(BF)
        count = length_ref[slot]
        kept = (lax.broadcasted_iota(jnp.int32, (PAD, 1), 0) < count).astype(F32)
        weight = kept * inv_std_of(centred) / count.astype(F32)
        pooled.append(jnp.sum(centred * weight, axis=0, keepdims=True) * gain_ref[...])
    pooled_ref[...] = jnp.concatenate(pooled, axis=0).astype(BF)


def split_core(core, rows, part, send_ref, keep_ref):
    run = 40
    for j in range(rows.shape[0] // (4 * run)):
        first = rows[j * 4 * run : j * 4 * run + run]
        second = rows[j * 4 * run + run : j * 4 * run + 2 * run]
        third = rows[j * 4 * run + 2 * run : j * 4 * run + 3 * run]
        fourth = rows[j * 4 * run + 3 * run : j * 4 * run + 4 * run]
        even = jnp.concatenate([first, third], axis=0)
        odd = jnp.concatenate([second, fourth], axis=0)
        base = part * rows.shape[0] // 2 + j * 2 * run
        span = slice(base, base + 2 * run)
        send_ref[span, :] = jnp.where(core == 0, odd, even).astype(BF)
        keep_ref[span, :] = jnp.where(core == 0, even, odd).astype(BF)


def hidden_kernel(
    core_ref, length_ref, h0, h1, h2, h3, h4, h5, h6, h7, pulled_ref, act_a_ref, act_b_ref,
    grad_ref, send_ref, keep_ref, hidden_ref, arrived,
):
    rows = h0.shape[0]
    pieces = [
        pltpu.make_async_copy(ref, hidden_ref.at[pl.ds(k * rows, rows)], arrived.at[k])
        for k, ref in enumerate((h0, h1, h2, h3, h4, h5, h6, h7))
    ]
    for piece in pieces:
        piece.start()
    for piece in pieces:
        piece.wait()

    def sample(index, carry):
        span = pl.ds(pl.multiple_of(index * PAD, PAD), PAD)
        centred = hidden_ref[span, :].astype(F32)
        inv = inv_std_of(centred)
        hat = centred * inv
        pulled = pulled_ref[pl.ds(index, 1), :]
        along = jnp.mean(pulled * hat, axis=-1, keepdims=True)
        count = length_ref[index]
        kept = (lax.broadcasted_iota(jnp.int32, (PAD, 1), 0) < count).astype(F32)
        weight = kept * inv / count.astype(F32)
        grad = weight * (pulled - jnp.mean(pulled, axis=-1, keepdims=True) - hat * along)
        grad_ref[span, :] = grad.astype(BF)
        return carry

    lax.fori_loop(0, grad_ref.shape[0] // PAD, sample, 0)
    tokens = act_a_ref.shape[0]
    for part in range(2):
        cols = slice(part * 640, (part + 1) * 640)
        rows = lax.dot_general(
            grad_ref[:tokens, cols], act_a_ref[...], OVER_ROWS, preferred_element_type=F32
        ) + lax.dot_general(
            grad_ref[tokens:, cols], act_b_ref[...], OVER_ROWS, preferred_element_type=F32
        )
        split_core(core_ref[0], rows, part, send_ref, keep_ref)


def weights_kernel(
    core_ref, grad_ref, down_ref, slope_a_ref, slope_b_ref, normed_a_ref, normed_b_ref,
    send_ref, keep_ref, scratch,
):
    tokens = slope_a_ref.shape[0]
    for part, slope_ref in enumerate((slope_a_ref, slope_b_ref)):
        span = slice(part * tokens, (part + 1) * tokens)
        back = lax.dot_general(
            grad_ref[span, :], down_ref[...], OVER_COLS, preferred_element_type=F32
        )
        scratch[span, :] = (back * slope_ref[...].astype(F32)).astype(BF)
    for part in range(2):
        cols = slice(part * 640, (part + 1) * 640)
        rows = lax.dot_general(
            normed_a_ref[:, cols], scratch[:tokens, :], OVER_ROWS, preferred_element_type=F32
        ) + lax.dot_general(
            normed_b_ref[:, cols], scratch[tokens:, :], OVER_ROWS, preferred_element_type=F32
        )
        split_core(core_ref[0], rows, part, send_ref, keep_ref)


def spread_y_kernel(y_ref, keep_ref, got_ref, own_ref, s1_ref, s2_ref, s3_ref, scratch):
    scratch[...] = keep_ref[...].astype(F32) + got_ref[...].astype(F32)
    for shift, ref in ((0, own_ref), (1, s1_ref), (3, s2_ref), (2, s3_ref)):
        place = lax.rem(y_ref[0] + shift, 4) * 40
        for pair in range(2):
            runs = [
                scratch[pl.ds(pl.multiple_of((2 * pair + k) * 160 + place, 8), 40), :]
                for k in range(2)
            ]
            ref[pair * 80 : (pair + 1) * 80, :] = jnp.concatenate(runs, axis=0).astype(ref.dtype)


def spread_z_kernel(z_ref, keep_ref, r1_ref, r2_ref, r3_ref, own_ref, s1_ref, s2_ref, s3_ref, scratch):
    scratch[...] = (
        keep_ref[...]
        + r1_ref[...].astype(F32)
        + r2_ref[...].astype(F32)
        + r3_ref[...].astype(F32)
    )
    for shift, ref in ((0, own_ref), (1, s1_ref), (3, s2_ref), (2, s3_ref)):
        place = lax.rem(z_ref[0] + shift, 4) * 40
        ref[...] = scratch[pl.ds(pl.multiple_of(place, 8), 40), :].astype(ref.dtype)


def move_txt(value, z_hi=0, x=0):
    pairs = [
        (a * 4 + b, ((a + z_hi) % 2) * 4 + (b + x) % 4) for a in range(2) for b in range(4)
    ]
    return lax.ppermute(value, "txt", pairs)


def move_img(value, z_lo=0, y=0, core=0):
    pairs = [
        (a * 8 + b * 2 + c, ((a + z_lo) % 4) * 8 + ((b + y) % 4) * 2 + (c + core) % 2)
        for a in range(4)
        for b in range(4)
        for c in range(2)
    ]
    return lax.ppermute(value, "img", pairs)


def nought(*events):
    return sum(event[0, 0].astype(F32) for event in events) * 0.0


def joined(*rows):
    return lax.optimization_barrier(jnp.concatenate(rows, axis=0))


def ring_txt(rows):
    return rows, move_txt(rows, x=1), move_txt(rows, x=-1), move_txt(rows, x=2)


def ring_z(rows):
    return rows, move_img(rows, z_lo=1), move_img(rows, z_lo=-1), move_img(rows, z_lo=2)


def ring_y(rows):
    return rows, move_img(rows, y=1), move_img(rows, y=-1), move_img(rows, y=2)


def gather_core(rows):
    return jnp.concatenate([rows, move_img(rows, core=1)], axis=0)


def ring_x(piece, way):
    left, right = move_txt(piece, x=1), move_txt(piece, x=-1)
    return piece, left, right, move_txt(left if way > 0 else right, x=way)


def ring_x_back(terms, held=None):
    own, left, right, far_a, far_b = terms
    got_a = move_txt(far_a, x=1)
    got_b = move_txt(far_b, x=-1)
    if held is not None:
        got_a, got_b, held = lax.optimization_barrier((got_a, got_b, held))
    left, right = call(
        relay_kernel, (shape(left.shape[0], left.shape[1], BF),) * 2, left, right, got_a, got_b
    )
    return (own, move_txt(right, x=1), move_txt(left, x=-1)), held


def forward(pieces, up_weight, down_weight):
    rows = pieces[0].shape[0]
    tokens = 4 * rows
    width, units = up_weight.shape
    return call(
        forward_kernel,
        (
            shape(tokens, width, BF),
            shape(tokens, units, BF),
            shape(tokens, units, BF),
            shape(tokens // PAD, width + 512, BF),
        )
        + (shape(rows, width, F32),) * 3
        + (shape(rows // 2, width, BF),) * 2,
        *pieces,
        up_weight,
        down_weight,
        flops=4 * tokens * width * units,
    )


def sum_img_start(send, keep, y):
    got = move_img(send, core=1)
    cols = keep.shape[1]
    outs = (shape(160, cols, F32),) + (shape(160, cols, BF),) * 3
    own, s1, s2, s3 = call(
        spread_y_kernel, outs, y, keep, got, scratch=[pltpu.VMEM(keep.shape, F32)], smem=1
    )
    return own, s1, s2, s3


def sum_img_end(terms, z_lo):
    own, s1, s2, s3 = terms
    cols = own.shape[1]
    s3, s1, s2 = move_img(s3, y=2), move_img(s1, y=1), move_img(s2, y=-1)
    outs = (shape(40, cols, F32),) + (shape(40, cols, BF),) * 3
    own, s1, s2, s3 = call(
        spread_z_kernel, outs, z_lo, own, s1, s2, s3,
        scratch=[pltpu.VMEM((160, cols), F32)], smem=1,
    )
    s3, s1, s2 = move_img(s3, z_lo=2), move_img(s1, z_lo=1), move_img(s2, z_lo=-1)
    return own + s1.astype(F32) + s2.astype(F32) + s3.astype(F32)


def body(
    text_states,
    text_length,
    sample_count,
    mlp_gain,
    up_weight,
    down_weight,
    final_gain,
    text_proj,
    image_pooled,
    image_gain,
    image_proj,
    logit_scale,
):
    samples, length, width = text_states.shape
    image_width = image_pooled.shape[1]
    txt = lax.axis_index("txt")
    img = lax.axis_index("img")
    z_lo, y, core = img // 8, (img // 2) % 4, img % 2

    row_gain = mlp_gain.reshape(1, width)
    row_final = final_gain.reshape(1, width)

    rows = samples * PAD
    padding = pltpu.VMEM((PAD, width), F32)
    (normed_own,) = call(
        norm_kernel,
        (shape(rows, width, BF),),
        sample_count,
        text_length,
        text_states,
        image_pooled,
        row_gain,
        scratch=[padding],
        smem=2,
    )
    near = ring_x(normed_own, 1)
    normed_far = move_txt(normed_own, z_hi=1) + nought(near[2]).astype(BF)
    away = ring_x(normed_far, -1)
    normed_near, act_near, slope_near, image_near, *terms_near = forward(
        near, up_weight, down_weight
    )
    normed_away, act_away, slope_away, image_away, *terms_away = forward(
        away, up_weight, down_weight
    )
    image_rows = jnp.concatenate([image_near, image_away], axis=0)
    image_rows = jnp.concatenate(ring_z(image_rows), axis=0)
    terms_away, image_rows = ring_x_back(terms_away, image_rows)
    terms_near, _ = ring_x_back(terms_near)
    (away_sum,) = call(away_kernel, (shape(rows, width, BF),), *terms_away)
    from_away, image_rows = lax.optimization_barrier(
        (move_txt(away_sum, z_hi=1), jnp.concatenate(ring_y(image_rows), axis=0))
    )

    pooled, hidden, half_a, half_b = call(
        final_kernel,
        (shape(samples, width, BF), shape(rows, width, BF)) + (shape(PAD, width, BF),) * 2,
        text_length,
        text_states,
        *terms_near,
        from_away,
        row_final,
        scratch=[padding],
        smem=1,
    )
    def together(*values):
        return lax.optimization_barrier(values)

    def rows_of(pieces):
        return jnp.concatenate(pieces, axis=0)

    pooled, hidden, half_a, half_b, image_rows = together(
        pooled, hidden, half_a, half_b, image_rows
    )
    pooled_x, left, right, half_a, half_b, image_all = together(
        rows_of(ring_txt(pooled)), move_txt(hidden, x=1), move_txt(hidden, x=-1), half_a, half_b,
        gather_core(image_rows),
    )
    pooled_txt, far, half_a, half_b, left, right, image_all = together(
        rows_of((pooled_x, move_txt(pooled_x, z_hi=1))), move_txt(left, x=1),
        move_txt(half_a, z_hi=1), half_b, left, right, image_all,
    )
    hidden_near = (hidden, left, right, far)
    pooled_z, hidden_far, image_all = together(
        rows_of(ring_z(pooled_txt)), rows_of((half_a, move_txt(half_b, z_hi=1))), image_all
    )
    pooled_y, far_left, far_right, hidden_far = together(
        rows_of(ring_y(pooled_z)),
        move_txt(hidden_far, x=1), move_txt(hidden_far, x=-1), hidden_far,
    )

    valid = image_all[:, image_width] > 0.5
    lengths = image_all[: 8 * samples, image_width + 1].astype(jnp.int32)
    image_centred = centre(image_all[:, :image_width].astype(F32))
    image_normed = (image_centred * inv_std_of(image_centred) * image_gain).astype(BF)
    image_raw = jnp.dot(image_normed, image_proj, preferred_element_type=F32)
    image_unit, image_inv = unit_rows(image_raw)
    image_send = image_unit.astype(BF)

    pooled_all = gather_core(pooled_y)

    group = 8 * samples
    text_raw = jnp.dot(pooled_all, text_proj, preferred_element_type=F32)
    text_inv = lax.rsqrt(jnp.sum(text_raw * text_raw, axis=-1, keepdims=True) + 1e-06)
    text_inv, far_far = together(text_inv, move_txt(far_right, x=-1))
    text_unit = text_raw * text_inv
    text_send = text_unit.astype(BF)
    hidden_away = (hidden_far, far_left, far_right, far_far)
    scores = logit_scale * lax.dot_general(
        text_send, image_send, OVER_COLS, preferred_element_type=F32
    )
    batch = scores.shape[0]

    def masked_logsum(axis, mask):
        top = jnp.max(jnp.where(mask, scores, -1e30), axis=axis, keepdims=True)
        total = jnp.sum(jnp.exp(jnp.where(mask, scores - top, -1e30)), axis=axis, keepdims=True)
        return top + jnp.log(total)

    row_lse = masked_logsum(0, valid[:, None])
    col_lse = masked_logsum(1, valid[None, :])
    pair_mask = valid[:, None] & valid[None, :]
    row_prob = jnp.exp(jnp.where(pair_mask, scores - row_lse, -1e30))
    col_prob = jnp.exp(jnp.where(pair_mask, scores - col_lse, -1e30))
    same = jnp.arange(batch)[:, None] == jnp.arange(batch)[None, :]
    grad_scores = 0.5 * (row_prob + col_prob) - jnp.where(pair_mask & same, 1.0, 0.0)
    grad_high = lax.reduce_precision(grad_scores, 8, 7)
    grad_low = (grad_scores - grad_high).astype(BF)
    grad_high = grad_high.astype(BF)

    grad_text_unit = logit_scale * (
        jnp.dot(grad_high[:group], image_send, preferred_element_type=F32)
        + jnp.dot(grad_low[:group], image_send, preferred_element_type=F32)
    )
    grad_text_raw = unit_back(grad_text_unit, text_unit[:group], text_inv[:group]).astype(BF)
    grad_pooled = lax.dot_general(
        grad_text_raw, text_proj, OVER_COLS, preferred_element_type=F32
    )
    pulled = grad_pooled * final_gain
    core_at, y_at, z_at = (v.reshape(1).astype(jnp.int32) for v in (core, y, z_lo))
    units = act_near.shape[1]
    tokens = group * PAD
    sums = (shape(width // 2, units, BF),) * 2
    grad_hidden, down_send, down_keep = call(
        hidden_kernel,
        (shape(tokens, width, BF),) + sums,
        core_at,
        lengths,
        *hidden_near,
        *hidden_away,
        pulled,
        act_near,
        act_away,
        scratch=[pltpu.VMEM((tokens, width), BF), pltpu.SemaphoreType.DMA((8,))],
        smem=2,
        anywhere=8,
        flops=2 * tokens * width * units,
    )
    up_send, up_keep = call(
        weights_kernel,
        sums,
        core_at,
        grad_hidden,
        down_weight,
        slope_near,
        slope_away,
        normed_near,
        normed_away,
        scratch=[pltpu.VMEM((tokens, units), BF)],
        smem=1,
        flops=4 * tokens * width * units,
    )
    down_terms = sum_img_start(down_send, down_keep, y_at)
    up_terms = sum_img_start(up_send, up_keep, y_at)
    down_grad = sum_img_end(down_terms, z_at).T
    up_grad = sum_img_end(up_terms, z_at)

    grad_image_unit = logit_scale * (
        lax.dot_general(grad_high, text_send, OVER_ROWS, preferred_element_type=F32)
        + lax.dot_general(grad_low, text_send, OVER_ROWS, preferred_element_type=F32)
    )
    grad_image_raw = unit_back(grad_image_unit, image_unit, image_inv).astype(BF)
    columns = grad_image_raw.shape[1] // 32
    chosen = jnp.arange(grad_image_raw.shape[1])[:, None] == (
        img * columns + jnp.arange(columns)[None, :]
    )
    own_columns = jnp.dot(
        grad_image_raw, chosen.astype(BF), preferred_element_type=F32
    ).astype(BF)
    projected = lax.dot_general(image_normed, own_columns, OVER_ROWS, preferred_element_type=F32)
    rows = image_width // 8
    image_proj_grad = lax.dynamic_slice_in_dim(projected, txt * rows, rows, axis=0)
    return (image_proj_grad, up_grad, down_grad)


def solution(mesh):
    return jax.shard_map(
        body,
        mesh=mesh,
        in_specs=(
            P(("img", "txt"), None, None),
            P(("img", "txt")),
            P(("img", "txt")),
            P(),
            P(None, "txt"),
            P("txt", None),
            P(),
            P(),
            P(("img", "txt"), None),
            P(),
            P(),
            P(),
        ),
        out_specs=(P("txt", "img"), P("img", "txt"), P("txt", "img")),
        check_vma=False,
    )
```

```python
import jax
import jax.numpy as jnp
from jax import lax
from jax.experimental import pallas as pl
from jax.experimental.pallas import tpu as pltpu
from jax.sharding import PartitionSpec as P

EPSILON = 1e-05
ROOT_HALF = 0.7071067811865476
INV_ROOT_TAU = 0.3989422804014327
BF = jnp.bfloat16
F32 = jnp.float32
PAD = 80


def centre(values):
    return values - jnp.mean(values, axis=-1, keepdims=True)


def inv_std_of(centred):
    return lax.rsqrt(jnp.mean(centred * centred, axis=-1, keepdims=True) + EPSILON)


def unit_rows(raw):
    inv_norm = lax.rsqrt(jnp.sum(raw * raw, axis=-1, keepdims=True) + 1e-06)
    return (raw * inv_norm, inv_norm)


def unit_back(grad_unit, direction, inv_norm):
    return inv_norm * (
        grad_unit - direction * jnp.sum(direction * grad_unit, axis=-1, keepdims=True)
    )


VMEM_LIMIT = 40 * 1024 * 1024
OVER_ROWS = (((0,), (0,)), ((), ()))
OVER_COLS = (((1,), (1,)), ((), ()))


def call(kernel, outs, *operands, scratch=(), smem=0, anywhere=0, flops=0):
    size = sum(v.size * v.dtype.itemsize for v in operands) + sum(
        v.size * v.dtype.itemsize for v in outs
    )
    specs = [pl.BlockSpec(memory_space=pltpu.SMEM)] * smem
    specs += [pl.BlockSpec(memory_space=pl.ANY)] * anywhere
    specs += [pl.BlockSpec(memory_space=pltpu.VMEM)] * (len(operands) - smem - anywhere)
    return pl.pallas_call(
        kernel,
        out_shape=outs,
        in_specs=specs,
        out_specs=[pl.BlockSpec(memory_space=pltpu.VMEM)] * len(outs),
        scratch_shapes=list(scratch),
        cost_estimate=pl.CostEstimate(flops=flops, bytes_accessed=size, transcendentals=0),
        compiler_params=pltpu.CompilerParams(vmem_limit_bytes=VMEM_LIMIT),
    )(*operands)


def shape(rows, cols, dtype):
    return jax.ShapeDtypeStruct((rows, cols), dtype)


def padded(states_ref, slot, scratch):
    length = states_ref.shape[1]
    scratch[PAD - 8 :, :] = jnp.zeros((8, scratch.shape[1]), F32)
    scratch[:length, :] = states_ref[slot].astype(F32)
    return scratch[...]


def norm_kernel(count_ref, length_ref, states_ref, image_ref, gain_ref, out_ref, scratch):
    length = states_ref.shape[1]
    width = out_ref.shape[1]
    rest = image_ref.shape[1] - width
    lane = lax.broadcasted_iota(jnp.int32, (1, 128), 1)
    image = image_ref[...].astype(F32)
    for slot in range(states_ref.shape[0]):
        centred = centre(padded(states_ref, slot, scratch))
        scratch[...] = centred * inv_std_of(centred) * gain_ref[...]
        valid = (slot < count_ref[0]).astype(F32)
        flags = jnp.where(lane == 0, valid, length_ref[slot].astype(F32))
        scratch[length : length + 1, :] = image[slot : slot + 1, :width]
        scratch[length + 1 : length + 2, :rest] = image[slot : slot + 1, width:]
        scratch[length + 1 : length + 2, rest : rest + 128] = jnp.where(lane < 2, flags, 0.0)
        out_ref[slot * PAD : (slot + 1) * PAD, :] = scratch[...].astype(BF)


def forward_kernel(
    own_ref, left_ref, right_ref, far_ref, up_ref, down_ref,
    normed_ref, act_ref, slope_ref, image_ref, o_own, o_left, o_right, o_far_a, o_far_b,
):
    rows = own_ref.shape[0]
    image = []
    for k, ref in enumerate((own_ref, left_ref, right_ref, far_ref)):
        normed_ref[k * rows : (k + 1) * rows, :] = ref[...]
        for end in range(PAD, rows + 1, PAD):
            last = ref[end - 16 : end, :].astype(F32)
            image.append(jnp.concatenate([last[13:14, :], last[14:15, :512]], axis=1))
    image_ref[...] = jnp.concatenate(image, axis=0).astype(BF)
    for part in range(2):
        span = slice(2 * part * rows, 2 * (part + 1) * rows)
        preact = jnp.dot(normed_ref[span, :], up_ref[...], preferred_element_type=F32)
        cdf = 0.5 * (1.0 + lax.erf(preact * ROOT_HALF))
        act_ref[span, :] = (preact * cdf).astype(BF)
        slope = cdf + preact * INV_ROOT_TAU * jnp.exp(-0.5 * preact * preact)
        slope_ref[span, :] = slope.astype(BF)
        out = jnp.dot(act_ref[span, :], down_ref[...], preferred_element_type=F32)
        if part == 0:
            o_own[...] = out[:rows]
            o_left[...] = out[rows:]
        else:
            o_right[...] = out[:rows]
            o_far_a[...] = out[rows : rows + rows // 2].astype(BF)
            o_far_b[...] = out[rows + rows // 2 :].astype(BF)


def relay_kernel(left_ref, right_ref, got_a_ref, got_b_ref, o_left, o_right):
    half = got_a_ref.shape[0]
    o_right[:half, :] = (right_ref[:half, :] + got_a_ref[...].astype(F32)).astype(BF)
    o_right[half:, :] = right_ref[half:, :].astype(BF)
    o_left[:half, :] = left_ref[:half, :].astype(BF)
    o_left[half:, :] = (left_ref[half:, :] + got_b_ref[...].astype(F32)).astype(BF)


def away_kernel(own_ref, left_ref, right_ref, out_ref):
    total = own_ref[...] + left_ref[...].astype(F32) + right_ref[...].astype(F32)
    out_ref[...] = total.astype(BF)


def final_kernel(
    length_ref, states_ref, own_ref, left_ref, right_ref, away_ref, gain_ref,
    pooled_ref, centred_ref, half_a_ref, half_b_ref, scratch,
):
    pooled = []
    for slot in range(states_ref.shape[0]):
        span = slice(slot * PAD, (slot + 1) * PAD)
        total = own_ref[span, :] + left_ref[span, :].astype(F32) + right_ref[span, :].astype(F32)
        total = total + away_ref[span, :].astype(F32)
        centred = centre(padded(states_ref, slot, scratch) + total)
        centred_ref[span, :] = centred.astype(BF)
        (half_a_ref, half_b_ref)[slot][...] = centred.astype(BF)
        count = length_ref[slot]
        kept = (lax.broadcasted_iota(jnp.int32, (PAD, 1), 0) < count).astype(F32)
        weight = kept * inv_std_of(centred) / count.astype(F32)
        pooled.append(jnp.sum(centred * weight, axis=0, keepdims=True) * gain_ref[...])
    pooled_ref[...] = jnp.concatenate(pooled, axis=0).astype(BF)


def split_core(core, rows, part, send_ref, keep_ref):
    run = 40
    for j in range(rows.shape[0] // (4 * run)):
        first = rows[j * 4 * run : j * 4 * run + run]
        second = rows[j * 4 * run + run : j * 4 * run + 2 * run]
        third = rows[j * 4 * run + 2 * run : j * 4 * run + 3 * run]
        fourth = rows[j * 4 * run + 3 * run : j * 4 * run + 4 * run]
        even = jnp.concatenate([first, third], axis=0)
        odd = jnp.concatenate([second, fourth], axis=0)
        base = part * rows.shape[0] // 2 + j * 2 * run
        span = slice(base, base + 2 * run)
        send_ref[span, :] = jnp.where(core == 0, odd, even).astype(BF)
        keep_ref[span, :] = jnp.where(core == 0, even, odd).astype(BF)


def hidden_kernel(
    core_ref, length_ref, h0, h1, h2, h3, h4, h5, h6, h7, pulled_ref, act_a_ref, act_b_ref,
    grad_ref, send_ref, keep_ref, hidden_ref, arrived,
):
    rows = h0.shape[0]
    pieces = [
        pltpu.make_async_copy(ref, hidden_ref.at[pl.ds(k * rows, rows)], arrived.at[k])
        for k, ref in enumerate((h0, h1, h2, h3, h4, h5, h6, h7))
    ]
    for piece in pieces:
        piece.start()
    for piece in pieces:
        piece.wait()

    def sample(index, carry):
        span = pl.ds(pl.multiple_of(index * PAD, PAD), PAD)
        centred = hidden_ref[span, :].astype(F32)
        inv = inv_std_of(centred)
        hat = centred * inv
        pulled = pulled_ref[pl.ds(index, 1), :]
        along = jnp.mean(pulled * hat, axis=-1, keepdims=True)
        count = length_ref[index]
        kept = (lax.broadcasted_iota(jnp.int32, (PAD, 1), 0) < count).astype(F32)
        weight = kept * inv / count.astype(F32)
        grad = weight * (pulled - jnp.mean(pulled, axis=-1, keepdims=True) - hat * along)
        grad_ref[span, :] = grad.astype(BF)
        return carry

    lax.fori_loop(0, grad_ref.shape[0] // PAD, sample, 0)
    tokens = act_a_ref.shape[0]
    for part in range(2):
        cols = slice(part * 640, (part + 1) * 640)
        rows = lax.dot_general(
            grad_ref[:tokens, cols], act_a_ref[...], OVER_ROWS, preferred_element_type=F32
        ) + lax.dot_general(
            grad_ref[tokens:, cols], act_b_ref[...], OVER_ROWS, preferred_element_type=F32
        )
        split_core(core_ref[0], rows, part, send_ref, keep_ref)


def weights_kernel(
    core_ref, grad_ref, down_ref, slope_a_ref, slope_b_ref, normed_a_ref, normed_b_ref,
    send_ref, keep_ref, scratch,
):
    tokens = slope_a_ref.shape[0]
    for part, slope_ref in enumerate((slope_a_ref, slope_b_ref)):
        span = slice(part * tokens, (part + 1) * tokens)
        back = lax.dot_general(
            grad_ref[span, :], down_ref[...], OVER_COLS, preferred_element_type=F32
        )
        scratch[span, :] = (back * slope_ref[...].astype(F32)).astype(BF)
    for part in range(2):
        cols = slice(part * 640, (part + 1) * 640)
        rows = lax.dot_general(
            normed_a_ref[:, cols], scratch[:tokens, :], OVER_ROWS, preferred_element_type=F32
        ) + lax.dot_general(
            normed_b_ref[:, cols], scratch[tokens:, :], OVER_ROWS, preferred_element_type=F32
        )
        split_core(core_ref[0], rows, part, send_ref, keep_ref)


def spread_y_kernel(y_ref, keep_ref, got_ref, own_ref, s1_ref, s2_ref, s3_ref, scratch):
    scratch[...] = keep_ref[...].astype(F32) + got_ref[...].astype(F32)
    for shift, ref in ((0, own_ref), (1, s1_ref), (3, s2_ref), (2, s3_ref)):
        place = lax.rem(y_ref[0] + shift, 4) * 40
        for pair in range(2):
            runs = [
                scratch[pl.ds(pl.multiple_of((2 * pair + k) * 160 + place, 8), 40), :]
                for k in range(2)
            ]
            ref[pair * 80 : (pair + 1) * 80, :] = jnp.concatenate(runs, axis=0).astype(ref.dtype)


def spread_z_kernel(z_ref, keep_ref, r1_ref, r2_ref, r3_ref, own_ref, s1_ref, s2_ref, s3_ref, scratch):
    scratch[...] = (
        keep_ref[...]
        + r1_ref[...].astype(F32)
        + r2_ref[...].astype(F32)
        + r3_ref[...].astype(F32)
    )
    for shift, ref in ((0, own_ref), (1, s1_ref), (3, s2_ref), (2, s3_ref)):
        place = lax.rem(z_ref[0] + shift, 4) * 40
        ref[...] = scratch[pl.ds(pl.multiple_of(place, 8), 40), :].astype(ref.dtype)


def move_txt(value, z_hi=0, x=0):
    pairs = [
        (a * 4 + b, ((a + z_hi) % 2) * 4 + (b + x) % 4) for a in range(2) for b in range(4)
    ]
    return lax.ppermute(value, "txt", pairs)


def move_img(value, z_lo=0, y=0, core=0):
    pairs = [
        (a * 8 + b * 2 + c, ((a + z_lo) % 4) * 8 + ((b + y) % 4) * 2 + (c + core) % 2)
        for a in range(4)
        for b in range(4)
        for c in range(2)
    ]
    return lax.ppermute(value, "img", pairs)


def nought(*events):
    return sum(event[0, 0].astype(F32) for event in events) * 0.0


def joined(*rows):
    return lax.optimization_barrier(jnp.concatenate(rows, axis=0))


def ring_txt(rows):
    return rows, move_txt(rows, x=1), move_txt(rows, x=-1), move_txt(rows, x=2)


def ring_z(rows):
    return rows, move_img(rows, z_lo=1), move_img(rows, z_lo=-1), move_img(rows, z_lo=2)


def ring_y(rows):
    return rows, move_img(rows, y=1), move_img(rows, y=-1), move_img(rows, y=2)


def gather_core(rows):
    return jnp.concatenate([rows, move_img(rows, core=1)], axis=0)


def ring_x(piece, way):
    left, right = move_txt(piece, x=1), move_txt(piece, x=-1)
    return piece, left, right, move_txt(left if way > 0 else right, x=way)


def ring_x_back(terms, held=None):
    own, left, right, far_a, far_b = terms
    got_a = move_txt(far_a, x=1)
    got_b = move_txt(far_b, x=-1)
    if held is not None:
        got_a, got_b, held = lax.optimization_barrier((got_a, got_b, held))
    left, right = call(
        relay_kernel, (shape(left.shape[0], left.shape[1], BF),) * 2, left, right, got_a, got_b
    )
    return (own, move_txt(right, x=1), move_txt(left, x=-1)), held


def forward(pieces, up_weight, down_weight):
    rows = pieces[0].shape[0]
    tokens = 4 * rows
    width, units = up_weight.shape
    return call(
        forward_kernel,
        (
            shape(tokens, width, BF),
            shape(tokens, units, BF),
            shape(tokens, units, BF),
            shape(tokens // PAD, width + 512, BF),
        )
        + (shape(rows, width, F32),) * 3
        + (shape(rows // 2, width, BF),) * 2,
        *pieces,
        up_weight,
        down_weight,
        flops=4 * tokens * width * units,
    )


def sum_img_start(send, keep, y):
    got = move_img(send, core=1)
    cols = keep.shape[1]
    outs = (shape(160, cols, F32),) + (shape(160, cols, BF),) * 3
    own, s1, s2, s3 = call(
        spread_y_kernel, outs, y, keep, got, scratch=[pltpu.VMEM(keep.shape, F32)], smem=1
    )
    return own, s1, s2, s3


def sum_img_end(terms, z_lo):
    own, s1, s2, s3 = terms
    cols = own.shape[1]
    s3, s1, s2 = move_img(s3, y=2), move_img(s1, y=1), move_img(s2, y=-1)
    outs = (shape(40, cols, F32),) + (shape(40, cols, BF),) * 3
    own, s1, s2, s3 = call(
        spread_z_kernel, outs, z_lo, own, s1, s2, s3,
        scratch=[pltpu.VMEM((160, cols), F32)], smem=1,
    )
    s3, s1, s2 = move_img(s3, z_lo=2), move_img(s1, z_lo=1), move_img(s2, z_lo=-1)
    return own + s1.astype(F32) + s2.astype(F32) + s3.astype(F32)


def body(
    text_states,
    text_length,
    sample_count,
    mlp_gain,
    up_weight,
    down_weight,
    final_gain,
    text_proj,
    image_pooled,
    image_gain,
    image_proj,
    logit_scale,
):
    samples, length, width = text_states.shape
    image_width = image_pooled.shape[1]
    txt = lax.axis_index("txt")
    img = lax.axis_index("img")
    z_lo, y, core = img // 8, (img // 2) % 4, img % 2

    row_gain = mlp_gain.reshape(1, width)
    row_final = final_gain.reshape(1, width)

    rows = samples * PAD
    padding = pltpu.VMEM((PAD, width), F32)
    (normed_own,) = call(
        norm_kernel,
        (shape(rows, width, BF),),
        sample_count,
        text_length,
        text_states,
        image_pooled,
        row_gain,
        scratch=[padding],
        smem=2,
    )
    near = ring_x(normed_own, 1)
    normed_far = move_txt(normed_own, z_hi=1) + nought(near[2]).astype(BF)
    away = ring_x(normed_far, -1)
    normed_near, act_near, slope_near, image_near, *terms_near = forward(
        near, up_weight, down_weight
    )
    normed_away, act_away, slope_away, image_away, *terms_away = forward(
        away, up_weight, down_weight
    )
    image_rows = jnp.concatenate([image_near, image_away], axis=0)
    image_rows = jnp.concatenate(ring_z(image_rows), axis=0)
    terms_away, image_rows = ring_x_back(terms_away, image_rows)
    terms_near, _ = ring_x_back(terms_near)
    (away_sum,) = call(away_kernel, (shape(rows, width, BF),), *terms_away)
    from_away, image_rows = lax.optimization_barrier(
        (move_txt(away_sum, z_hi=1), jnp.concatenate(ring_y(image_rows), axis=0))
    )

    pooled, hidden, half_a, half_b = call(
        final_kernel,
        (shape(samples, width, BF), shape(rows, width, BF)) + (shape(PAD, width, BF),) * 2,
        text_length,
        text_states,
        *terms_near,
        from_away,
        row_final,
        scratch=[padding],
        smem=1,
    )
    def together(*values):
        return lax.optimization_barrier(values)

    def rows_of(pieces):
        return jnp.concatenate(pieces, axis=0)

    pooled, hidden, half_a, half_b, image_rows = together(
        pooled, hidden, half_a, half_b, image_rows
    )
    left, right = move_txt(hidden, x=1), move_txt(hidden, x=-1)
    pooled_x, left, right, half_a, half_b, image_all = together(
        rows_of(ring_txt(pooled)), left, right, move_txt(half_a, z_hi=1), half_b,
        gather_core(image_rows),
    )
    pooled_txt, far, hidden_far, left, right = together(
        rows_of((pooled_x, move_txt(pooled_x, z_hi=1))), move_txt(left, x=1),
        rows_of((half_a, move_txt(half_b, z_hi=1))), left, right,
    )
    hidden_near = (hidden, left, right, far)
    pooled_z, far_left, far_right, hidden_far = together(
        rows_of(ring_z(pooled_txt)),
        move_txt(hidden_far, x=1), move_txt(hidden_far, x=-1), hidden_far,
    )
    pooled_y, far_far, far_left, far_right, hidden_far = together(
        rows_of(ring_y(pooled_z)), move_txt(far_right, x=-1), far_left, far_right, hidden_far
    )
    hidden_away = (hidden_far, far_left, far_right, far_far)

    valid = image_all[:, image_width] > 0.5
    lengths = image_all[: 8 * samples, image_width + 1].astype(jnp.int32)
    image_centred = centre(image_all[:, :image_width].astype(F32))
    image_normed = (image_centred * inv_std_of(image_centred) * image_gain).astype(BF)
    (image_normed,) = together(image_normed)
    image_raw = jnp.dot(image_normed, image_proj, preferred_element_type=F32)
    image_unit, image_inv = unit_rows(image_raw)
    image_send = image_unit.astype(BF)
    image_low = (image_unit - lax.reduce_precision(image_unit, 8, 7)).astype(BF)

    pooled_all = gather_core(pooled_y)

    group = 8 * samples
    text_raw = jnp.dot(pooled_all, text_proj, preferred_element_type=F32)
    text_unit, text_inv = unit_rows(text_raw)
    text_send = text_unit.astype(BF)
    scores = logit_scale * lax.dot_general(
        text_send, image_send, OVER_COLS, preferred_element_type=F32
    )
    batch = scores.shape[0]

    def masked_logsum(axis, mask):
        top = jnp.max(jnp.where(mask, scores, -1e30), axis=axis, keepdims=True)
        total = jnp.sum(jnp.exp(jnp.where(mask, scores - top, -1e30)), axis=axis, keepdims=True)
        return top + jnp.log(total)

    row_lse = masked_logsum(0, valid[:, None])
    col_lse = masked_logsum(1, valid[None, :])
    pair_mask = valid[:, None] & valid[None, :]
    row_prob = jnp.exp(jnp.where(pair_mask, scores - row_lse, -1e30))
    col_prob = jnp.exp(jnp.where(pair_mask, scores - col_lse, -1e30))
    same = jnp.arange(batch)[:, None] == jnp.arange(batch)[None, :]
    grad_scores = 0.5 * (row_prob + col_prob) - jnp.where(pair_mask & same, 1.0, 0.0)
    grad_high = lax.reduce_precision(grad_scores, 8, 7)
    grad_low = (grad_scores - grad_high).astype(BF)
    grad_high = grad_high.astype(BF)

    grad_text_unit = logit_scale * (
        jnp.dot(grad_high[:group], image_send, preferred_element_type=F32)
        + jnp.dot(grad_low[:group], image_send, preferred_element_type=F32)
    )
    grad_text_raw = unit_back(grad_text_unit, text_unit[:group], text_inv[:group]).astype(BF)
    grad_pooled = lax.dot_general(
        grad_text_raw, text_proj, OVER_COLS, preferred_element_type=F32
    )
    pulled = grad_pooled * final_gain
    core_at, y_at, z_at = (v.reshape(1).astype(jnp.int32) for v in (core, y, z_lo))
    units = act_near.shape[1]
    tokens = group * PAD
    sums = (shape(width // 2, units, BF),) * 2
    grad_hidden, down_send, down_keep = call(
        hidden_kernel,
        (shape(tokens, width, BF),) + sums,
        core_at,
        lengths,
        *hidden_near,
        *hidden_away,
        pulled,
        act_near,
        act_away,
        scratch=[pltpu.VMEM((tokens, width), BF), pltpu.SemaphoreType.DMA((8,))],
        smem=2,
        anywhere=8,
        flops=2 * tokens * width * units,
    )
    up_send, up_keep = call(
        weights_kernel,
        sums,
        core_at,
        grad_hidden,
        down_weight,
        slope_near,
        slope_away,
        normed_near,
        normed_away,
        scratch=[pltpu.VMEM((tokens, units), BF)],
        smem=1,
        flops=4 * tokens * width * units,
    )
    down_terms = sum_img_start(down_send, down_keep, y_at)
    up_terms = sum_img_start(up_send, up_keep, y_at)
    down_grad = sum_img_end(down_terms, z_at).T
    up_grad = sum_img_end(up_terms, z_at)

    columns = image_unit.shape[1] // 32
    chosen = jnp.arange(image_unit.shape[1])[:, None] == (
        img * columns + jnp.arange(columns)[None, :]
    )
    chosen = chosen.astype(BF)
    pick_columns = (((0,), (1,)), ((), ()))
    text_columns = lax.dot_general(
        chosen, text_send, pick_columns, preferred_element_type=F32
    ).astype(BF)
    unit_columns = lax.dot_general(
        chosen, image_send, pick_columns, preferred_element_type=F32
    ) + lax.dot_general(chosen, image_low, pick_columns, preferred_element_type=F32)
    rest = logit_scale * lax.dot_general(
        text_send, image_low, OVER_COLS, preferred_element_type=F32
    )
    along = jnp.sum(grad_scores * (scores + rest), axis=0, keepdims=True)
    grad_columns = logit_scale * (
        jnp.dot(text_columns, grad_high, preferred_element_type=F32)
        + jnp.dot(text_columns, grad_low, preferred_element_type=F32)
    )
    own_columns = (image_inv.reshape(1, batch) * (grad_columns - unit_columns * along)).astype(BF)
    projected = lax.dot_general(
        image_normed, own_columns, (((0,), (1,)), ((), ())), preferred_element_type=F32
    )
    rows = image_width // 8
    image_proj_grad = lax.dynamic_slice_in_dim(projected, txt * rows, rows, axis=0)
    return (image_proj_grad, up_grad, down_grad)


def solution(mesh):
    return jax.shard_map(
        body,
        mesh=mesh,
        in_specs=(
            P(("img", "txt"), None, None),
            P(("img", "txt")),
            P(("img", "txt")),
            P(),
            P(None, "txt"),
            P("txt", None),
            P(),
            P(),
            P(("img", "txt"), None),
            P(),
            P(),
            P(),
        ),
        out_specs=(P("txt", "img"), P("img", "txt"), P("txt", "img")),
        check_vma=False,
    )
```
